128 devices in a mesh: slab: 16 (over y, x), sub: 8 (over z, core).
Axes of the slice: x: 4, y: 4, z: 4, core: 2. Of those that a mesh axis runs over, the one named last changes fastest.
Arguments:
- ref_pos: float32 [3, 1048576], P(None, ('slab', 'sub')), may hold values from 0 to 1
- disp: float32 [3, 1048576], P(None, ('slab', 'sub')), may hold values from -0.3 to 0.3
- vel: float32 [3, 1048576], P(None, ('slab', 'sub')), may hold values from -0.6 to 0.6
- pressure: float32 [1024, 1024], P('slab', 'sub'), may hold values from 0.2 to 1.5
- conductivity: float32 [1024, 1024], P('slab', 'sub'), may hold values from 0.02 to 0.2
- frac_mask: int32 [1024, 1024], P('slab', 'sub'), may hold values 0 or 1
- send_list: int32 [2048, 32], P(('slab', 'sub')), may hold values from 0 to 63
- pair_list: int32 [32768, 2], P(('slab', 'sub')), may hold values from 0 to 511
- pair_count: int32 [128], P(('slab', 'sub')), may hold values from 128 to 256, as said below
- bond_flags: int32 [32768, 10, 128], P(('slab', 'sub')), may hold values from 0 to 16383, as said below
Outputs:
- disp_out: float32 [3, 1048576], P(None, ('slab', 'sub'))
- vel_out: float32 [3, 1048576], P(None, ('slab', 'sub'))
- pressure_out: float32 [1024, 1024], P('slab', 'sub')
The draws below stay inside these ranges and needn't reach their ends.
Inputs may be any that keep to these rules, and one draw needn't show every extreme that they name: send_list entries are local block numbers of the sending device; pair_list entries number received copies as sender position * 32 + slot. `pair_count`: one device in every draw holds exactly 256 live pair slots. `bond_flags`: the flag of bond (a, b) is bit a % 14 of word a // 14 in column b; bits beyond 128 rows are zero.
All inputs are finite; a program needn't handle non-finite values. No bound on the sum of `frac_mask` on one device may be relied on, other than what follows from the above.
Results may differ from the reference program's by a relative error of at most 0.0003.
Values sent between devices are 32-bit elements; how exact they have to be, the bound alone decides.
A program may use at most 64 MiB of HBM per device.

```python
import math
import jax
import jax.numpy as jnp
from jax import lax

BLOCK = 128
NB_DEV = 64
CAP = 32
PAIRS_DEV = 256
CY = 128
STEPS = 2
WORDS = 10
CX = 64
NX = 1024
NY = 1024
POINTS = 1048576
BLOCKS = 8192
PAIRS = 32768
SLOTS = 512
N_SLAB = 16
N_SUB = 8
DEVICES = 128


def draw_pair_count(key, part):
    key = jax.random.fold_in(key, 11)
    first_key, second_key = jax.random.split(key)
    counts = jax.random.randint(first_key, (DEVICES,), PAIRS_DEV // 2, PAIRS_DEV + 1, dtype=jnp.int32)
    fullest = jax.random.randint(second_key, (), 0, DEVICES, dtype=jnp.int32)
    return counts.at[fullest].set(PAIRS_DEV)


def draw_bond_flags(key, part):
    key = jax.random.fold_in(key, 23)
    packed = jax.random.randint(key, (PAIRS, WORDS, BLOCK), 0, 2 ** 14, dtype=jnp.int32)
    live_bits = jnp.clip(BLOCK - 14 * jnp.arange(WORDS, dtype=jnp.int32), 0, 14)
    limit = jnp.left_shift(jnp.ones((WORDS,), jnp.int32), live_bits) - 1
    return jnp.bitwise_and(packed, limit[None, :, None])


def with_ends(drawn, rng, smallest, largest):
    longest = drawn.shape.index(max(drawn.shape))
    spots = []
    for shift in (0, 1):
        where = [jax.random.randint(jax.random.fold_in(rng, axis), (), 0, length) for axis, length in enumerate(drawn.shape)]
        where[longest] = (where[longest] + shift) % drawn.shape[longest]
        spots.append(tuple(where))
    return drawn.at[spots[0]].set(smallest).at[spots[1]].set(largest)


def steps_of(stream_key, extent, pieces, low, high):
    factor_of = 1.0
    for axis_at, blocks in pieces:
        steps = jax.random.uniform(jax.random.fold_in(jax.random.fold_in(stream_key, 6), axis_at), (blocks,), jnp.float32, low / len(pieces), high / len(pieces))
        factor_of = factor_of * jnp.repeat(jnp.exp(steps), extent[axis_at] // blocks).reshape((-1,) + (1,) * (len(extent) - 1 - axis_at))
    return factor_of


def scatter_about(stream_key, extent, scale, reach, shards=(), kind=jnp.bfloat16):
    values = jax.random.normal(stream_key, extent, jnp.float32) * scale
    if len(shards) > 0:
        values = steps_of(stream_key, extent, shards, -0.22, 0.18) * values
    return jnp.clip(values, min=-reach, max=reach).astype(kind)


def setup_inputs(seed: int = 0) -> dict:
    splits = jax.random.split(jax.random.key(seed), 11)
    return {
        "ref_pos": jnp.clip(1.0 * jax.random.uniform(splits[0], (3, POINTS), jnp.float32) ** steps_of(splits[0], (3, POINTS), ((1, 128),), -0.2, 0.2), 0.0, 1.0),
        "disp": scatter_about(splits[1], (3, POINTS), 0.05, 0.3, ((1, 128),), jnp.float32),
        "vel": scatter_about(splits[2], (3, POINTS), 0.1, 0.6, ((1, 128),), jnp.float32),
        "pressure": jnp.clip(0.2 + 1.3 * jax.random.uniform(splits[3], (NX, NY), jnp.float32) ** steps_of(splits[3], (NX, NY), ((0, 16), (1, 8)), -0.2, 0.2), 0.2, 1.5),
        "conductivity": jnp.clip(jnp.exp(math.log(0.2) - 2.3025851 * jax.random.uniform(splits[4], (NX, NY), jnp.float32) ** steps_of(splits[4], (NX, NY), ((0, 16), (1, 8)), -0.2, 0.2)), 0.02, 0.2),
        "frac_mask": with_ends((jax.random.randint(splits[5], (NX, NY), 0, 2) < 1).astype(jnp.int32), jax.random.fold_in(splits[5], 1), 0, 1),
        "send_list": with_ends(jax.random.randint(splits[6], (N_SLAB * N_SUB * N_SLAB, CAP), 0, NB_DEV), jax.random.fold_in(splits[6], 1), 0, NB_DEV - 1).astype(jnp.int32),
        "pair_list": with_ends(jax.random.randint(splits[7], (PAIRS, 2), 0, SLOTS), jax.random.fold_in(splits[7], 1), 0, SLOTS - 1).astype(jnp.int32),
        "pair_count": draw_pair_count(jax.random.fold_in(splits[10], 71), 0),
        "bond_flags": draw_bond_flags(jax.random.fold_in(splits[10], 71), 0),
    }


soft_sq = 0.0025
reach_sq = 0.09
stiffness = 4.0
pressure_coupling = 0.3
time_step = 0.2
flow_step = 1.0

def unpack_flags(packed, width):
    shifts = jnp.arange(14, dtype=jnp.int32)
    spread = jnp.bitwise_and(jnp.right_shift(packed[:, :, None, :], shifts[None, None, :, None]), 1)
    spread = spread.reshape(packed.shape[0], packed.shape[1] * 14, packed.shape[2])
    return spread[:, :width, :].astype(jnp.float32)

def tile_forces(start_first, start_second, moving_first, moving_second, packed, alive):
    offset = start_second[:, :, None, :] - start_first[:, :, :, None]
    stretched = offset + moving_second[:3, :, None, :] - moving_first[:3, :, :, None]
    rest_sq = lax.optimization_barrier(jnp.sum(offset * offset, axis=0))
    rest_len = jnp.sqrt(rest_sq + soft_sq)
    now_len = jnp.sqrt(lax.optimization_barrier(jnp.sum(stretched * stretched, axis=0)) + soft_sq)
    influence = reach_sq / (reach_sq + rest_sq)
    mean_pressure = 0.5 * (moving_first[3][:, :, None] + moving_second[3][:, None, :])
    flags = unpack_flags(packed, offset.shape[-1])
    factor = stiffness * flags * alive[:, None, None] * influence * ((now_len - rest_len) / rest_len - pressure_coupling * mean_pressure) / now_len
    bond_force = factor[None] * stretched
    return (lax.optimization_barrier(jnp.sum(bond_force, axis=3)), -lax.optimization_barrier(jnp.sum(bond_force, axis=2)))

def flow(centre, padded, wet, conduct, rock):
    total = jnp.zeros_like(centre)
    for shift_row, shift_col in ((1, 0), (-1, 0), (0, 1), (0, -1)):
        rows = slice(1 + shift_row, padded.shape[0] - 1 + shift_row)
        cols = slice(1 + shift_col, padded.shape[1] - 1 + shift_col)
        face = 0.5 * (conduct * wet * rock[0, rows, cols] + rock[1, rows, cols] * wet)
        total = total + face * (padded[rows, cols] - centre)
    return centre + flow_step * total

def to_points(grid):
    return grid.reshape(N_SLAB, CX, N_SUB, CY).transpose(0, 2, 1, 3).reshape(POINTS)

def reference(ref_pos, disp, vel, pressure, conductivity, frac_mask, send_list, pair_list, pair_count, bond_flags):
    wet = frac_mask.astype(jnp.float32)
    pair_index = jnp.arange(PAIRS, dtype=jnp.int32)
    device_of = pair_index // PAIRS_DEV
    slab_of = device_of // N_SUB
    sub_of = device_of % N_SUB

    def global_block(slot_entry):
        sender = slot_entry // CAP * N_SUB + sub_of
        local_block = send_list[sender * N_SLAB + slab_of, slot_entry % CAP]
        return (sender * NB_DEV + local_block).astype(jnp.int32)
    first_block = global_block(pair_list[:, 0])
    second_block = global_block(pair_list[:, 1])
    live = (pair_index % PAIRS_DEV < pair_count[device_of]).astype(jnp.float32)
    rock = jnp.pad(jnp.stack([wet, conductivity * wet]), ((0, 0), (1, 1), (1, 1)))
    group = math.gcd(PAIRS, 64)
    for step_index in range(STEPS):
        wet_points = to_points(pressure * wet)
        start_blocks = ref_pos.reshape(3, BLOCKS, BLOCK)
        moving_blocks = jnp.concatenate([disp, wet_points[None]], axis=0).reshape(4, BLOCKS, BLOCK)

        def one_group(index):
            first = lax.dynamic_slice_in_dim(first_block, index * group, group, 0)
            second = lax.dynamic_slice_in_dim(second_block, index * group, group, 0)
            packed = lax.dynamic_slice_in_dim(bond_flags, index * group, group, 0)
            alive = lax.dynamic_slice_in_dim(live, index * group, group, 0)
            return tile_forces(start_blocks[:, first], start_blocks[:, second], moving_blocks[:, first], moving_blocks[:, second], packed, alive)
        on_first, on_second = lax.map(one_group, jnp.arange(PAIRS // group, dtype=jnp.int32))
        on_first = on_first.transpose(1, 0, 2, 3).reshape(3, PAIRS, BLOCK)
        on_second = on_second.transpose(1, 0, 2, 3).reshape(3, PAIRS, BLOCK)
        force = jnp.zeros((3, BLOCKS, BLOCK), jnp.float32)
        force = force.at[:, first_block].add(on_first).at[:, second_block].add(on_second)
        pressure = flow(pressure, jnp.pad(pressure, 1), wet, conductivity, rock)
        vel = vel + time_step * force.reshape(3, POINTS)
        disp = disp + time_step * vel
    return (disp, vel, pressure)
```

```python
import functools

import jax
import jax.numpy as jnp
from jax import lax
from jax.experimental import pallas as pl
from jax.experimental.pallas import tpu as pltpu
from jax.sharding import PartitionSpec as P

MESH = pl.DeviceIdType.MESH
F32 = jnp.float32
BF16 = jnp.bfloat16

STEPS = 2
SOFT = 0.0025
REACH = 0.09
COUPLING = 0.3
DT = 0.2
FORCE_SCALE = 4.0 * REACH
FLOW = 1.0

NB = 64
CAP = 32
PAIRS = 256
SIDE = 4
PEERS = SIDE * SIDE
GROUP = 8
OFFSETS = [(dy, dx) for dy in range(SIDE) for dx in range(SIDE)]


def dot(a, b, ca=1, cb=0):
    return lax.dot_general(a, b, (((ca,), (cb,)), ((), ())), preferred_element_type=F32)


def split(t):
    high = t.astype(BF16)
    rest = t - high.astype(F32)
    mid = rest.astype(BF16)
    low = (rest - mid.astype(F32)).astype(BF16)
    return high, mid, low


def stack(parts):
    return jnp.concatenate(parts, axis=0)


def pair_rows(first, second, with_pressure):
    row = lax.broadcasted_iota(jnp.int32, (8, 128), 0)
    coord = row < 3
    centre = jnp.where(coord, jnp.broadcast_to(first[:, 0:1], (8, 128)), 0.0)
    a = first - centre
    b = second - centre
    norm_a = jnp.sum(jnp.where(coord, a * a, 0.0), axis=0, keepdims=True) + SOFT
    norm_b = jnp.sum(jnp.where(coord, b * b, 0.0), axis=0, keepdims=True)
    left = jnp.where(coord, a, jnp.where(row == 3, norm_a, jnp.where(row == 5, 1.0, 0.0)))
    right = jnp.where(coord, -2.0 * b, jnp.where(row == 3, 1.0, jnp.where(row == 5, norm_b, 0.0)))
    load = None
    if with_pressure:
        left = jnp.where(row == 4, first[3:4, :], left)
        load = jnp.where(row == 4, 1.0, jnp.where(row == 5, second[3:4, :], 0.0))
    return a, b, left, right, load


def six_left(parts):
    h, m, l = parts
    return stack([h, h, m, m, h, l])


def six_right(parts):
    h, m, l = parts
    return stack([h, m, h, m, l, h])


def tile_at(ref, slot):
    return ref[slot]


def rest_group(ks, pair_s, slots_ref, flags_ref, c1_ref, c2_ref):
    squares = []
    for k in ks:
        _, _, left, right, _ = pair_rows(
            tile_at(slots_ref, pair_s[0, k]), tile_at(slots_ref, pair_s[1, k]), False
        )
        squares.append((six_left(split(left)), six_right(split(right))))
    squares = [dot(left, right, 0, 0) for left, right in squares]
    sub = lax.broadcasted_iota(jnp.int32, (8, 128), 0)
    for k, square in zip(ks, squares):
        for t in range(16):
            w0, w1 = (8 * t) // 14, (8 * t + 7) // 14
            word = jnp.broadcast_to(flags_ref[w0, pl.ds(k, 1), :], (8, 128))
            if w1 != w0:
                other = jnp.broadcast_to(flags_ref[w1, pl.ds(k, 1), :], (8, 128))
                word = jnp.where(sub < (14 * w1 - 8 * t), word, other)
            bit = lax.shift_left(jnp.int32(1), lax.rem(sub + 8 * t, 14))
            value = jnp.maximum(square[8 * t : 8 * t + 8, :], SOFT)
            inverse = lax.rsqrt(value)
            q = lax.rsqrt(value + (REACH - SOFT))
            c2 = jnp.where(jnp.bitwise_and(word, bit) != 0, q * q, 0.0)
            c1_ref[k, pl.ds(8 * t, 8), :] = c2 * inverse
            c2_ref[k, pl.ds(8 * t, 8), :] = c2


def move_group(ks, pair_s, slots_ref, c1_ref, c2_ref, on_ref):
    pre = []
    for k in ks:
        a, b, left, right, load = pair_rows(
            tile_at(slots_ref, pair_s[0, k]), tile_at(slots_ref, pair_s[1, k]), True
        )
        ls, rs, ps = split(left), split(right), split(load)
        wide = jnp.concatenate([six_right(rs), six_right(ps)], axis=1)
        pre.append((a, b, six_left(ls), wide, stack(ls), stack(rs)))
    products = [dot(p[2], p[3], 0, 0) for p in pre]
    factors = []
    for k, product in zip(ks, products):
        highs, lows = [], []
        for t in range(8):
            rows = slice(16 * t, 16 * t + 16)
            square = jnp.maximum(product[rows, :128], SOFT)
            load = product[rows, 128:]
            f = c1_ref[k, pl.ds(16 * t, 16), :] - c2_ref[k, pl.ds(16 * t, 16), :] * (
                load * lax.rsqrt(square)
            )
            high = f.astype(BF16)
            highs.append(high)
            lows.append((f - high.astype(F32)).astype(BF16))
        factors.append((stack(highs), stack(lows)))
    sums = []
    for p, (high, low) in zip(pre, factors):
        sums.append(
            (dot(p[5], high, 1, 1) + dot(p[5], low, 1, 1), dot(p[4], high) + dot(p[4], low))
        )
    for k, p, (ga, gb) in zip(ks, pre, sums):
        ga = ga[0:8] + ga[8:16] + ga[16:24]
        gb = gb[0:8] + gb[8:16] + gb[16:24]
        on_a = -0.5 * ga - p[0] * ga[3:4, :]
        on_b = gb - p[1] * gb[5:6, :]
        on_ref[pl.ds(k, 3, stride=2 * PAIRS), :] = on_a[0:3]
        on_ref[pl.ds(PAIRS + k, 3, stride=2 * PAIRS), :] = on_b[0:3]


def kernel(
    pair_s, count_s, ref, disp, vel, pres, cond, mask, send_v, pair_v, flags_any,
    disp_o, vel_o, pres_o,
    flags, rest, shift, speed, owner, chooser, slots_rest, slots_move, on, c1, c2,
    ref_out, ref_in, mov_out0, mov_out1, mov_in0, mov_in1, frc_out0, frc_out1, frc_in0, frc_in1,
    cells0, cells1, west0, east0, west1, east1, north0, south0, north1, south1,
    face_n, face_s, face_w, face_e, press, wet,
    flag_sem, send_sem, recv_sem, halo_send, halo_recv,
):
    s = lax.axis_index("slab")
    u = lax.axis_index("sub")
    slabs = lax.axis_size("slab")
    subs = lax.axis_size("sub")
    y, x = s // SIDE, s % SIDE
    peer = {o: ((y + o[0]) % SIDE) * SIDE + (x + o[1]) % SIDE for o in OFFSETS}
    up, down = (s + slabs - 1) % slabs, (s + 1) % slabs
    left, right = (u + subs - 1) % subs, (u + 1) % subs

    barrier = pltpu.get_barrier_semaphore()
    for o in OFFSETS[1:]:
        pl.semaphore_signal(barrier, inc=1, device_id=(peer[o], u), device_id_type=MESH)
    for v in (left, right):
        pl.semaphore_signal(barrier, inc=1, device_id=(s, v), device_id_type=MESH)
    flag_copy = pltpu.make_async_copy(flags_any, flags, flag_sem)
    flag_copy.start()

    for l in range(NB):
        lanes = slice(128 * l, 128 * l + 128)
        r = ref[:, lanes]
        rest[pl.ds(l, 3, stride=NB), :] = r
        shift[pl.ds(l, 3, stride=NB), :] = disp[:, lanes]
        speed[pl.ds(l, 3, stride=NB), :] = vel[:, lanes]
    wet[...] = mask[...].astype(F32)
    press[...] = pres[...]
    slots_rest[...] = jnp.zeros_like(slots_rest)
    slots_move[...] = jnp.zeros_like(slots_move)
    chosen = jnp.concatenate([send_v[p : p + 1, :] for p in range(PEERS)], axis=1)
    block = lax.broadcasted_iota(jnp.int32, (NB, PEERS * CAP), 0)
    table = jnp.where(chosen == block, 1.0, 0.0)
    owner[...] = table.astype(BF16)
    chooser[...] = jnp.transpose(table).astype(BF16)

    def fields(buffer, count):
        return [buffer[f * NB : (f + 1) * NB, :] for f in range(count)]

    def placed():
        return [r + d for r, d in zip(fields(rest, 3), fields(shift, 3))]

    def remote(src, dst, phase, n, o):
        return pltpu.make_async_remote_copy(
            src_ref=src.at[peer[o]],
            dst_ref=dst.at[s],
            send_sem=send_sem.at[phase, n],
            recv_sem=recv_sem.at[phase, n],
            device_id=(peer[o], u),
            device_id_type=MESH,
        )

    def send_row(src, dst, phase, dy):
        copies = []
        for n, o in enumerate(OFFSETS):
            if o[0] == dy and o != (0, 0):
                copy = remote(src, dst, phase, n, o)
                copy.start()
                copies.append(copy)
        return copies

    def distribute(values, src, dst, phase):
        parts = split(jnp.concatenate(values, axis=1))
        copies = []
        for dy in (1, 2, 3, 0):
            row = (y + dy) % SIDE
            pick = chooser[pl.ds(pl.multiple_of(row * SIDE * CAP, SIDE * CAP), SIDE * CAP), :]
            picked = dot(pick, parts[0]) + dot(pick, parts[1]) + dot(pick, parts[2])
            for q in range(SIDE):
                for f in range(len(values)):
                    src[row * SIDE + q, pl.ds(f * CAP, CAP), :] = picked[
                        q * CAP : (q + 1) * CAP, f * 128 : (f + 1) * 128
                    ]
            copies += send_row(src, dst, phase, dy)
        dst[s] = src[s]
        return copies

    def spread(src, dst, count):
        @pl.loop(0, PEERS)
        def _(p):
            for g in range(CAP // 8):
                for f in range(count):
                    dst[pl.ds(p * CAP + 8 * g, 8), f, :] = src[p, pl.ds(f * CAP + 8 * g, 8), :]

    def halo(src, n, dev, dst):
        return pltpu.make_async_remote_copy(
            src_ref=src, dst_ref=dst, send_sem=halo_send.at[n], recv_sem=halo_recv.at[n],
            device_id=dev, device_id_type=MESH,
        )

    cells0[0] = pres[...]
    cells0[1] = wet[...]
    cells0[2] = cond[...] * wet[...]
    pl.semaphore_wait(barrier, PEERS - 1 + 2)

    rest_copies = distribute(fields(rest, 3), ref_out, ref_in, 0)

    def load_of(pressure):
        return 0.5 + (0.5 * COUPLING) * (pressure * wet[...])

    move_copies = distribute(placed() + [load_of(press[...])], mov_out0, mov_in0, 1)

    halos = [
        halo(cells0.at[:, pl.ds(56, 8)], 0, (down, u), north0),
        halo(cells0.at[:, pl.ds(0, 8)], 1, (up, u), south0),
        halo(cells0, 2, (s, right), west0),
        halo(cells0, 3, (s, left), east0),
    ]
    for copy in halos:
        copy.start()

    for copy in rest_copies:
        copy.wait_recv()
    spread(ref_in, slots_rest, 3)
    flag_copy.wait()

    @pl.loop(0, PAIRS // GROUP)
    def _(j):
        rest_group(
            [j * GROUP + d for d in range(GROUP)], pair_s, slots_rest, flags, c1, c2
        )

    for copy in move_copies:
        copy.wait_recv()

    rows = lax.broadcasted_iota(jnp.int32, (64, 128), 0)
    lanes = lax.broadcasted_iota(jnp.int32, (64, 128), 1)

    def neighbours(centre, north, south, west, east):
        return (
            jnp.where(rows == 0, north[7:8, :], pltpu.roll(centre, 1, 0)),
            jnp.where(rows == 63, south[0:1, :], pltpu.roll(centre, 63, 0)),
            jnp.where(lanes == 0, pltpu.roll(west, 1, 1), pltpu.roll(centre, 1, 1)),
            jnp.where(lanes == 127, pltpu.roll(east, 127, 1), pltpu.roll(centre, 127, 1)),
        )

    def faces():
        inside = (
            jnp.logical_or(rows > 0, s > 0),
            jnp.logical_or(rows < 63, s < slabs - 1),
            jnp.logical_or(lanes > 0, u > 0),
            jnp.logical_or(lanes < 127, u < subs - 1),
        )
        wets = neighbours(wet[...], north0[1], south0[1], west0[1], east0[1])
        rocks = neighbours(cells0[2], north0[2], south0[2], west0[2], east0[2])
        for face, ok, w, r in zip((face_n, face_s, face_w, face_e), inside, wets, rocks):
            value = 0.5 * (cond[...] * wet[...] * w + r * wet[...])
            face[...] = jnp.where(ok, value, 0.0)

    def flow(north, south, west, east):
        centre = press[...]
        total = jnp.zeros_like(centre)
        around = neighbours(centre, north, south, west, east)
        for face, value in zip((face_s, face_n, face_e, face_w), (1, 0, 3, 2)):
            total = total + face[...] * (around[value] - centre)
        press[...] = centre + FLOW * total

    def pair_forces(mov_in):
        spread(mov_in, slots_move, 4)

        @pl.loop(0, PAIRS // GROUP)
        def _(j):
            move_group([j * GROUP + d for d in range(GROUP)], pair_s, slots_move, c1, c2, on)

    live = lax.broadcasted_iota(jnp.int32, (2, PAIRS), 1) < count_s[0]
    named = jnp.where(live, pair_v[...], -1)
    ends = jnp.concatenate([named[0:1, :], named[1:2, :]], axis=1)

    def give_back(src, dst, phase):
        parts = split(
            jnp.concatenate([on[f * 2 * PAIRS : (f + 1) * 2 * PAIRS, :] for f in range(3)], axis=1)
        )
        copies = []
        for dy in (1, 2, 3, 0):
            row = (y + dy) % SIDE
            slot = lax.broadcasted_iota(jnp.int32, (SIDE * CAP, 2 * PAIRS), 0) + row * (SIDE * CAP)
            hit = jnp.where(slot == ends, 1.0, 0.0).astype(BF16)
            total = dot(hit, parts[0]) + dot(hit, parts[1]) + dot(hit, parts[2])
            for q in range(SIDE):
                for f in range(3):
                    src[row * SIDE + q, pl.ds(f * CAP, CAP), :] = total[
                        q * CAP : (q + 1) * CAP, f * 128 : (f + 1) * 128
                    ]
            copies += send_row(src, dst, phase, dy)
        dst[s] = src[s]
        return copies

    def advance(frc_in):
        parts = split(
            jnp.concatenate(
                [
                    frc_in[:, f * CAP : (f + 1) * CAP, :].reshape(PEERS * CAP, 128)
                    for f in range(3)
                ],
                axis=1,
            )
        )
        table = owner[...]
        force = dot(table, parts[0]) + dot(table, parts[1]) + dot(table, parts[2])
        for f in range(3):
            part = slice(f * NB, (f + 1) * NB)
            v = speed[part, :] + (DT * FORCE_SCALE) * force[:, f * 128 : (f + 1) * 128]
            speed[part, :] = v
            shift[part, :] = shift[part, :] + DT * v

    pair_forces(mov_in0)
    back_copies = give_back(frc_out0, frc_in0, 2)
    for copy in halos:
        copy.wait_recv()
    faces()
    flow(north0[0], south0[0], west0[0], east0[0])
    cells1[...] = press[...]
    halos1 = [
        halo(cells1.at[pl.ds(56, 8)], 4, (down, u), north1),
        halo(cells1.at[pl.ds(0, 8)], 5, (up, u), south1),
        halo(cells1, 6, (s, right), west1),
        halo(cells1, 7, (s, left), east1),
    ]
    for copy in halos1:
        copy.start()
    for copy in back_copies:
        copy.wait_recv()
    advance(frc_in0)

    next_copies = distribute(placed() + [load_of(press[...])], mov_out1, mov_in1, 3)
    for copy in halos1:
        copy.wait_recv()
    flow(north1[...], south1[...], west1[...], east1[...])
    pres_o[...] = press[...]
    for copy in next_copies:
        copy.wait_recv()
    pair_forces(mov_in1)
    last_copies = give_back(frc_out1, frc_in1, 4)
    for copy in last_copies:
        copy.wait_recv()
    advance(frc_in1)
    for l in range(NB):
        lanes_l = slice(128 * l, 128 * l + 128)
        disp_o[:, lanes_l] = shift[pl.ds(l, 3, stride=NB), :]
        vel_o[:, lanes_l] = speed[pl.ds(l, 3, stride=NB), :]
    for copies in (rest_copies, move_copies, halos, back_copies, halos1, next_copies, last_copies):
        for copy in copies:
            copy.wait_send()


def body(ref_pos, disp, vel, pressure, conductivity, frac_mask, send_list, pair_list, pair_count, bond_flags):
    vmem = pl.BlockSpec(memory_space=pltpu.VMEM)
    smem = pl.BlockSpec(memory_space=pltpu.SMEM)
    pairs = pair_list.T
    grid = pltpu.VMEM((64, 128), F32)
    three = pltpu.VMEM((3 * NB, 128), F32)
    third = pltpu.VMEM((PEERS, 3 * CAP, 128), F32)
    fourth = pltpu.VMEM((PEERS, 4 * CAP, 128), F32)
    slots = pltpu.VMEM((PEERS * CAP, 8, 128), F32)
    grids = pltpu.VMEM((3, 64, 128), F32)
    strips = pltpu.VMEM((3, 8, 128), F32)
    strip = pltpu.VMEM((8, 128), F32)
    tiles = pltpu.VMEM((PAIRS, 128, 128), F32)
    return pl.pallas_call(
        kernel,
        out_shape=(
            jax.ShapeDtypeStruct(disp.shape, F32),
            jax.ShapeDtypeStruct(vel.shape, F32),
            jax.ShapeDtypeStruct(pressure.shape, F32),
        ),
        in_specs=[smem, smem] + [vmem] * 8 + [pl.BlockSpec(memory_space=pl.ANY)],
        out_specs=(vmem, vmem, vmem),
        scratch_shapes=[
            pltpu.VMEM((10, PAIRS, 128), jnp.int32),
            three, three, three,
            pltpu.VMEM((NB, PEERS * CAP), BF16),
            pltpu.VMEM((PEERS * CAP, NB), BF16),
            slots, slots,
            pltpu.VMEM((3 * 2 * PAIRS, 128), F32),
            tiles, tiles,
            third, third, fourth, fourth, fourth, fourth, third, third, third, third,
            grids, grid, grids, grids, grid, grid, strips, strips, strip, strip,
            grid, grid, grid, grid, grid, grid,
            pltpu.SemaphoreType.DMA,
            pltpu.SemaphoreType.DMA((5, PEERS)),
            pltpu.SemaphoreType.DMA((5, PEERS)),
            pltpu.SemaphoreType.DMA((8,)),
            pltpu.SemaphoreType.DMA((8,)),
        ],
        compiler_params=pltpu.CompilerParams(
            collective_id=0, has_side_effects=True, vmem_limit_bytes=58 << 20
        ),
    )(
        pairs, pair_count, ref_pos, disp, vel, pressure, conductivity, frac_mask, send_list, pairs,
        bond_flags.transpose(1, 0, 2),
    )


def solution(mesh):
    in_specs = (
        P(None, ("slab", "sub")),
        P(None, ("slab", "sub")),
        P(None, ("slab", "sub")),
        P("slab", "sub"),
        P("slab", "sub"),
        P("slab", "sub"),
        P(("slab", "sub"), None),
        P(("slab", "sub"), None),
        P(("slab", "sub")),
        P(("slab", "sub"), None, None),
    )
    out_specs = (P(None, ("slab", "sub")), P(None, ("slab", "sub")), P("slab", "sub"))
    return jax.shard_map(body, mesh=mesh, in_specs=in_specs, out_specs=out_specs, check_vma=False)
```

```python
import functools

import jax
import jax.numpy as jnp
from jax import lax
from jax.experimental import pallas as pl
from jax.experimental.pallas import tpu as pltpu
from jax.sharding import PartitionSpec as P

MESH = pl.DeviceIdType.MESH
F32 = jnp.float32
BF16 = jnp.bfloat16

STEPS = 2
SOFT = 0.0025
REACH = 0.09
COUPLING = 0.3
DT = 0.2
FORCE_SCALE = 4.0 * REACH
FLOW = 1.0

NB = 64
CAP = 32
PAIRS = 256
SIDE = 4
PEERS = SIDE * SIDE
GROUP = 8
REST_GROUP = 16
OFFSETS = [(dy, dx) for dy in range(SIDE) for dx in range(SIDE)]


def dot(a, b, ca=1, cb=0):
    return lax.dot_general(a, b, (((ca,), (cb,)), ((), ())), preferred_element_type=F32)


def split(t):
    high = t.astype(BF16)
    rest = t - high.astype(F32)
    mid = rest.astype(BF16)
    low = (rest - mid.astype(F32)).astype(BF16)
    return high, mid, low


def stack(parts):
    return jnp.concatenate(parts, axis=0)


def pair_rows(first, second, with_pressure):
    row = lax.broadcasted_iota(jnp.int32, (8, 128), 0)
    coord = row < 3
    centre = jnp.where(coord, jnp.broadcast_to(first[:, 0:1], (8, 128)), 0.0)
    a = first - centre
    b = second - centre
    norm_a = jnp.sum(jnp.where(coord, a * a, 0.0), axis=0, keepdims=True) + SOFT
    norm_b = jnp.sum(jnp.where(coord, b * b, 0.0), axis=0, keepdims=True)
    left = jnp.where(coord, a, jnp.where(row == 3, norm_a, jnp.where(row == 5, 1.0, 0.0)))
    right = jnp.where(coord, -2.0 * b, jnp.where(row == 3, 1.0, jnp.where(row == 5, norm_b, 0.0)))
    load = None
    if with_pressure:
        left = jnp.where(row == 4, first[3:4, :], left)
        load = jnp.where(row == 4, 1.0, jnp.where(row == 5, second[3:4, :], 0.0))
    return a, b, left, right, load


def six_left(parts):
    h, m, l = parts
    return stack([h, h, m, m, h, l])


def six_right(parts):
    h, m, l = parts
    return stack([h, m, h, m, l, h])


def tile_at(ref, slot):
    return ref[slot]


def rest_group(ks, pair_s, slots_ref, flags_ref, c1_ref, c2_ref):
    squares = []
    for k in ks:
        _, _, left, right, _ = pair_rows(
            tile_at(slots_ref, pair_s[0, k]), tile_at(slots_ref, pair_s[1, k]), False
        )
        squares.append((six_left(split(left)), six_right(split(right))))
    squares = [dot(left, right, 0, 0) for left, right in squares]
    sub = lax.broadcasted_iota(jnp.int32, (8, 128), 0)
    for k, square in zip(ks, squares):
        for t in range(16):
            w0, w1 = (8 * t) // 14, (8 * t + 7) // 14
            word = jnp.broadcast_to(flags_ref[w0, pl.ds(k, 1), :], (8, 128))
            if w1 != w0:
                other = jnp.broadcast_to(flags_ref[w1, pl.ds(k, 1), :], (8, 128))
                word = jnp.where(sub < (14 * w1 - 8 * t), word, other)
            bit = lax.shift_left(jnp.int32(1), lax.rem(sub + 8 * t, 14))
            value = jnp.maximum(square[8 * t : 8 * t + 8, :], SOFT)
            inverse = lax.rsqrt(value)
            q = lax.rsqrt(value + (REACH - SOFT))
            c2 = jnp.where(jnp.bitwise_and(word, bit) != 0, q * q, 0.0)
            c1_ref[k, pl.ds(8 * t, 8), :] = c2 * inverse
            c2_ref[k, pl.ds(8 * t, 8), :] = c2


def bond_factors(buffer, ks, pair_s, slots_ref, c1_ref, c2_ref, factor, coords, tiles):
    pre = []
    for d, k in enumerate(ks):
        a, b, left, right, load = pair_rows(
            tile_at(slots_ref, pair_s[0, k]), tile_at(slots_ref, pair_s[1, k]), True
        )
        ls, rs, ps = split(left), split(right), split(load)
        pre.append((six_left(ls), jnp.concatenate([six_right(rs), six_right(ps)], axis=1)))
        coords[buffer, d, 0] = stack(ls[:2])
        coords[buffer, d, 1] = stack(rs[:2])
        tiles[buffer, d, 0] = a
        tiles[buffer, d, 1] = b
    products = [dot(left, right, 0, 0) for left, right in pre]
    for d, (k, product) in enumerate(zip(ks, products)):
        for t in range(8):
            rows = slice(16 * t, 16 * t + 16)
            square = jnp.maximum(product[rows, :128], SOFT)
            load = product[rows, 128:]
            f = c1_ref[k, pl.ds(16 * t, 16), :] - c2_ref[k, pl.ds(16 * t, 16), :] * (
                load * lax.rsqrt(square)
            )
            high = f.astype(BF16)
            factor[buffer, d, 0, rows, :] = high
            factor[buffer, d, 1, rows, :] = (f - high.astype(F32)).astype(BF16)


def bond_sums(buffer, ks, on_ref, factor, coords, tiles):
    sums = []
    for d in range(len(ks)):
        ca, cb = coords[buffer, d, 0], coords[buffer, d, 1]
        high, low = factor[buffer, d, 0], factor[buffer, d, 1]
        sums.append(
            (
                dot(
                    jnp.concatenate([cb, cb], axis=1),
                    jnp.concatenate([high, low], axis=1), 1, 1,
                ),
                dot(jnp.concatenate([ca, ca], axis=1), stack([high, low])),
            )
        )
    for d, (k, (ga, gb)) in enumerate(zip(ks, sums)):
        ga = ga[0:8] + ga[8:16]
        gb = gb[0:8] + gb[8:16]
        on_a = -0.5 * ga - tiles[buffer, d, 0] * ga[3:4, :]
        on_b = gb - tiles[buffer, d, 1] * gb[5:6, :]
        on_ref[pl.ds(k, 3, stride=2 * PAIRS), :] = on_a[0:3]
        on_ref[pl.ds(PAIRS + k, 3, stride=2 * PAIRS), :] = on_b[0:3]


def kernel(
    pair_s, count_s, ref, disp, vel, pres, cond, mask, send_v, pair_v, flags_any,
    state,
    flags, rest, shift, speed, owner, chooser, slots_rest, slots_move, on, c1, c2,
    factor, coords, tiles,
    ref_out, ref_in, mov_out0, mov_out1, mov_in0, mov_in1, frc_out0, frc_out1, frc_in0, frc_in1,
    cells0, cells1, west0, east0, west1, east1, north0, south0, north1, south1,
    face_n, face_s, face_w, face_e, press, wet,
    flag_sem, send_sem, recv_sem, halo_send, halo_recv,
):
    s = lax.axis_index("slab")
    u = lax.axis_index("sub")
    slabs = lax.axis_size("slab")
    subs = lax.axis_size("sub")
    y, x = s // SIDE, s % SIDE
    peer = {o: ((y + o[0]) % SIDE) * SIDE + (x + o[1]) % SIDE for o in OFFSETS}
    up, down = (s + slabs - 1) % slabs, (s + 1) % slabs
    left, right = (u + subs - 1) % subs, (u + 1) % subs

    barrier = pltpu.get_barrier_semaphore()
    for o in OFFSETS[1:]:
        pl.semaphore_signal(barrier, inc=1, device_id=(peer[o], u), device_id_type=MESH)
    for v in (left, right):
        pl.semaphore_signal(barrier, inc=1, device_id=(s, v), device_id_type=MESH)
    flag_copy = pltpu.make_async_copy(flags_any, flags, flag_sem)
    flag_copy.start()

    for l in range(NB):
        lanes = slice(128 * l, 128 * l + 128)
        r = ref[:, lanes]
        rest[pl.ds(l, 3, stride=NB), :] = r
        shift[pl.ds(l, 3, stride=NB), :] = disp[:, lanes]
        speed[pl.ds(l, 3, stride=NB), :] = vel[:, lanes]
    wet[...] = mask[...].astype(F32)
    press[...] = pres[...]
    slots_rest[...] = jnp.zeros_like(slots_rest)
    slots_move[...] = jnp.zeros_like(slots_move)
    chosen = jnp.concatenate([send_v[p : p + 1, :] for p in range(PEERS)], axis=1)
    block = lax.broadcasted_iota(jnp.int32, (NB, PEERS * CAP), 0)
    table = jnp.where(chosen == block, 1.0, 0.0)
    owner[...] = table.astype(BF16)
    chooser[...] = jnp.transpose(table).astype(BF16)

    def fields(buffer, count):
        return [buffer[f * NB : (f + 1) * NB, :] for f in range(count)]

    def placed():
        return [r + d for r, d in zip(fields(rest, 3), fields(shift, 3))]

    def remote(src, dst, phase, n, o):
        return pltpu.make_async_remote_copy(
            src_ref=src.at[peer[o]],
            dst_ref=dst.at[s],
            send_sem=send_sem.at[phase, n],
            recv_sem=recv_sem.at[phase, n],
            device_id=(peer[o], u),
            device_id_type=MESH,
        )

    def send_row(src, dst, phase, dy):
        copies = []
        for n, o in enumerate(OFFSETS):
            if o[0] == dy and o != (0, 0):
                copy = remote(src, dst, phase, n, o)
                copy.start()
                copies.append(copy)
        return copies

    def distribute(values, src, dst, phase):
        parts = split(jnp.concatenate(values, axis=1))
        copies = []
        for dy in (1, 2, 3, 0):
            row = (y + dy) % SIDE
            pick = chooser[pl.ds(pl.multiple_of(row * SIDE * CAP, SIDE * CAP), SIDE * CAP), :]
            picked = dot(pick, parts[0]) + dot(pick, parts[1]) + dot(pick, parts[2])
            for q in range(SIDE):
                for f in range(len(values)):
                    src[row * SIDE + q, pl.ds(f * CAP, CAP), :] = picked[
                        q * CAP : (q + 1) * CAP, f * 128 : (f + 1) * 128
                    ]
            copies += send_row(src, dst, phase, dy)
        dst[s] = src[s]
        return copies

    def spread(src, dst, count):
        @pl.loop(0, PEERS)
        def _(p):
            for g in range(CAP // 8):
                for f in range(count):
                    dst[pl.ds(p * CAP + 8 * g, 8), f, :] = src[p, pl.ds(f * CAP + 8 * g, 8), :]

    def halo(src, n, dev, dst):
        return pltpu.make_async_remote_copy(
            src_ref=src, dst_ref=dst, send_sem=halo_send.at[n], recv_sem=halo_recv.at[n],
            device_id=dev, device_id_type=MESH,
        )

    cells0[0] = pres[...]
    cells0[1] = wet[...]
    cells0[2] = cond[...] * wet[...]
    pl.semaphore_wait(barrier, PEERS - 1 + 2)

    rest_copies = distribute(fields(rest, 3), ref_out, ref_in, 0)

    def load_of(pressure):
        return 0.5 + (0.5 * COUPLING) * (pressure * wet[...])

    move_copies = distribute(placed() + [load_of(press[...])], mov_out0, mov_in0, 1)

    halos = [
        halo(cells0.at[:, pl.ds(56, 8)], 0, (down, u), north0),
        halo(cells0.at[:, pl.ds(0, 8)], 1, (up, u), south0),
        halo(cells0, 2, (s, right), west0),
        halo(cells0, 3, (s, left), east0),
    ]
    for copy in halos:
        copy.start()

    for copy in rest_copies:
        copy.wait_recv()
    spread(ref_in, slots_rest, 3)
    flag_copy.wait()

    @pl.loop(0, PAIRS // REST_GROUP)
    def _(j):
        rest_group(
            [j * REST_GROUP + d for d in range(REST_GROUP)], pair_s, slots_rest, flags, c1, c2
        )

    for copy in move_copies:
        copy.wait_recv()

    rows = lax.broadcasted_iota(jnp.int32, (64, 128), 0)
    lanes = lax.broadcasted_iota(jnp.int32, (64, 128), 1)

    def neighbours(centre, north, south, west, east):
        return (
            jnp.where(rows == 0, north[7:8, :], pltpu.roll(centre, 1, 0)),
            jnp.where(rows == 63, south[0:1, :], pltpu.roll(centre, 63, 0)),
            jnp.where(lanes == 0, pltpu.roll(west, 1, 1), pltpu.roll(centre, 1, 1)),
            jnp.where(lanes == 127, pltpu.roll(east, 127, 1), pltpu.roll(centre, 127, 1)),
        )

    def faces():
        inside = (
            jnp.logical_or(rows > 0, s > 0),
            jnp.logical_or(rows < 63, s < slabs - 1),
            jnp.logical_or(lanes > 0, u > 0),
            jnp.logical_or(lanes < 127, u < subs - 1),
        )
        wets = neighbours(wet[...], north0[1], south0[1], west0[1], east0[1])
        rocks = neighbours(cells0[2], north0[2], south0[2], west0[2], east0[2])
        for face, ok, w, r in zip((face_n, face_s, face_w, face_e), inside, wets, rocks):
            value = 0.5 * (cond[...] * wet[...] * w + r * wet[...])
            face[...] = jnp.where(ok, value, 0.0)

    def flow(north, south, west, east):
        centre = press[...]
        total = jnp.zeros_like(centre)
        around = neighbours(centre, north, south, west, east)
        for face, value in zip((face_s, face_n, face_e, face_w), (1, 0, 3, 2)):
            total = total + face[...] * (around[value] - centre)
        press[...] = centre + FLOW * total

    def pair_forces(mov_in):
        spread(mov_in, slots_move, 4)

        def members(j):
            return [j * GROUP + d for d in range(GROUP)]

        def make(buffer, j):
            bond_factors(buffer, members(j), pair_s, slots_move, c1, c2, factor, coords, tiles)

        def add(buffer, j):
            bond_sums(buffer, members(j), on, factor, coords, tiles)

        groups = PAIRS // GROUP
        make(0, 0)

        @pl.loop(0, groups // 2 - 1)
        def _(i):
            add(0, 2 * i)
            make(1, 2 * i + 1)
            add(1, 2 * i + 1)
            make(0, 2 * i + 2)

        add(0, groups - 2)
        make(1, groups - 1)
        add(1, groups - 1)

    live = lax.broadcasted_iota(jnp.int32, (2, PAIRS), 1) < count_s[0]
    named = jnp.where(live, pair_v[...], -1)
    ends = jnp.concatenate([named[0:1, :], named[1:2, :]], axis=1)

    def give_back(src, dst, phase):
        parts = split(
            jnp.concatenate([on[f * 2 * PAIRS : (f + 1) * 2 * PAIRS, :] for f in range(3)], axis=1)
        )
        copies = []
        for dy in (1, 2, 3, 0):
            row = (y + dy) % SIDE
            slot = lax.broadcasted_iota(jnp.int32, (SIDE * CAP, 2 * PAIRS), 0) + row * (SIDE * CAP)
            hit = jnp.where(slot == ends, 1.0, 0.0).astype(BF16)
            total = dot(hit, parts[0]) + dot(hit, parts[1]) + dot(hit, parts[2])
            for q in range(SIDE):
                for f in range(3):
                    src[row * SIDE + q, pl.ds(f * CAP, CAP), :] = total[
                        q * CAP : (q + 1) * CAP, f * 128 : (f + 1) * 128
                    ]
            copies += send_row(src, dst, phase, dy)
        dst[s] = src[s]
        return copies

    def advance(frc_in):
        parts = split(
            jnp.concatenate(
                [
                    frc_in[:, f * CAP : (f + 1) * CAP, :].reshape(PEERS * CAP, 128)
                    for f in range(3)
                ],
                axis=1,
            )
        )
        table = owner[...]
        force = dot(table, parts[0]) + dot(table, parts[1]) + dot(table, parts[2])
        for f in range(3):
            part = slice(f * NB, (f + 1) * NB)
            v = speed[part, :] + (DT * FORCE_SCALE) * force[:, f * 128 : (f + 1) * 128]
            speed[part, :] = v
            shift[part, :] = shift[part, :] + DT * v

    pair_forces(mov_in0)
    back_copies = give_back(frc_out0, frc_in0, 2)
    for copy in halos:
        copy.wait_recv()
    faces()
    flow(north0[0], south0[0], west0[0], east0[0])
    cells1[...] = press[...]
    halos1 = [
        halo(cells1.at[pl.ds(56, 8)], 4, (down, u), north1),
        halo(cells1.at[pl.ds(0, 8)], 5, (up, u), south1),
        halo(cells1, 6, (s, right), west1),
        halo(cells1, 7, (s, left), east1),
    ]
    for copy in halos1:
        copy.start()
    for copy in back_copies:
        copy.wait_recv()
    advance(frc_in0)

    next_copies = distribute(placed() + [load_of(press[...])], mov_out1, mov_in1, 3)
    for copy in halos1:
        copy.wait_recv()
    flow(north1[...], south1[...], west1[...], east1[...])
    for copy in next_copies:
        copy.wait_recv()
    pair_forces(mov_in1)
    last_copies = give_back(frc_out1, frc_in1, 4)
    for copy in last_copies:
        copy.wait_recv()
    advance(frc_in1)
    state[0 : 3 * NB, :] = shift[...]
    state[3 * NB : 6 * NB, :] = speed[...]
    state[6 * NB :, :] = press[...]
    for copies in (rest_copies, move_copies, halos, back_copies, halos1, next_copies, last_copies):
        for copy in copies:
            copy.wait_send()


def unpack_kernel(state, disp_o, vel_o, pres_o):
    for l in range(NB):
        lanes = slice(128 * l, 128 * l + 128)
        disp_o[:, lanes] = state[pl.ds(l, 3, stride=NB), :]
        vel_o[:, lanes] = state[pl.ds(3 * NB + l, 3, stride=NB), :]
    pres_o[...] = state[6 * NB :, :]


def body(ref_pos, disp, vel, pressure, conductivity, frac_mask, send_list, pair_list, pair_count, bond_flags):
    vmem = pl.BlockSpec(memory_space=pltpu.VMEM)
    smem = pl.BlockSpec(memory_space=pltpu.SMEM)
    pairs = pair_list.T
    grid = pltpu.VMEM((64, 128), F32)
    three = pltpu.VMEM((3 * NB, 128), F32)
    third = pltpu.VMEM((PEERS, 3 * CAP, 128), F32)
    fourth = pltpu.VMEM((PEERS, 4 * CAP, 128), F32)
    slots = pltpu.VMEM((PEERS * CAP, 8, 128), F32)
    grids = pltpu.VMEM((3, 64, 128), F32)
    strips = pltpu.VMEM((3, 8, 128), F32)
    strip = pltpu.VMEM((8, 128), F32)
    bonds = pltpu.VMEM((PAIRS, 128, 128), F32)
    state = pl.pallas_call(
        kernel,
        out_shape=jax.ShapeDtypeStruct((7 * NB, 128), F32),
        in_specs=[smem, smem] + [vmem] * 8 + [pl.BlockSpec(memory_space=pl.ANY)],
        out_specs=vmem,
        scratch_shapes=[
            pltpu.VMEM((10, PAIRS, 128), jnp.int32),
            three, three, three,
            pltpu.VMEM((NB, PEERS * CAP), BF16),
            pltpu.VMEM((PEERS * CAP, NB), BF16),
            slots, slots,
            pltpu.VMEM((3 * 2 * PAIRS, 128), F32),
            bonds, bonds,
            pltpu.VMEM((2, GROUP, 2, 128, 128), BF16),
            pltpu.VMEM((2, GROUP, 2, 16, 128), BF16),
            pltpu.VMEM((2, GROUP, 2, 8, 128), F32),
            third, third, fourth, fourth, fourth, fourth, third, third, third, third,
            grids, grid, grids, grids, grid, grid, strips, strips, strip, strip,
            grid, grid, grid, grid, grid, grid,
            pltpu.SemaphoreType.DMA,
            pltpu.SemaphoreType.DMA((5, PEERS)),
            pltpu.SemaphoreType.DMA((5, PEERS)),
            pltpu.SemaphoreType.DMA((8,)),
            pltpu.SemaphoreType.DMA((8,)),
        ],
        compiler_params=pltpu.CompilerParams(
            collective_id=0, has_side_effects=True, vmem_limit_bytes=58 << 20
        ),
    )(
        pairs, pair_count, ref_pos, disp, vel, pressure, conductivity, frac_mask, send_list, pairs,
        bond_flags.transpose(1, 0, 2),
    )
    return pl.pallas_call(
        unpack_kernel,
        out_shape=(
            jax.ShapeDtypeStruct(disp.shape, F32),
            jax.ShapeDtypeStruct(vel.shape, F32),
            jax.ShapeDtypeStruct(pressure.shape, F32),
        ),
        in_specs=[vmem],
        out_specs=(vmem, vmem, vmem),
    )(state)


def solution(mesh):
    in_specs = (
        P(None, ("slab", "sub")),
        P(None, ("slab", "sub")),
        P(None, ("slab", "sub")),
        P("slab", "sub"),
        P("slab", "sub"),
        P("slab", "sub"),
        P(("slab", "sub"), None),
        P(("slab", "sub"), None),
        P(("slab", "sub")),
        P(("slab", "sub"), None, None),
    )
    out_specs = (P(None, ("slab", "sub")), P(None, ("slab", "sub")), P("slab", "sub"))
    return jax.shard_map(body, mesh=mesh, in_specs=in_specs, out_specs=out_specs, check_vma=False)
```

```python
import functools

import jax
import jax.numpy as jnp
from jax import lax
from jax.experimental import pallas as pl
from jax.experimental.pallas import tpu as pltpu
from jax.sharding import PartitionSpec as P

MESH = pl.DeviceIdType.MESH
F32 = jnp.float32
BF16 = jnp.bfloat16

STEPS = 2
SOFT = 0.0025
REACH = 0.09
COUPLING = 0.3
DT = 0.2
FORCE_SCALE = 4.0 * REACH
FLOW = 1.0

NB = 64
CAP = 32
PAIRS = 256
SIDE = 4
PEERS = SIDE * SIDE
GROUP = 8
REST_GROUP = 16
ORDER = [
    (0, 1), (1, 0), (0, 3), (3, 0), (1, 1), (3, 3), (1, 3), (3, 1),
    (0, 2), (2, 0), (1, 2), (2, 1), (3, 2), (2, 3), (2, 2),
]


def dot(a, b, ca=1, cb=0):
    return lax.dot_general(a, b, (((ca,), (cb,)), ((), ())), preferred_element_type=F32)


def split(t):
    high = t.astype(BF16)
    rest = t - high.astype(F32)
    mid = rest.astype(BF16)
    low = (rest - mid.astype(F32)).astype(BF16)
    return high, mid, low


def stack(parts):
    return jnp.concatenate(parts, axis=0)


def pair_rows(first, second, with_pressure):
    row = lax.broadcasted_iota(jnp.int32, (8, 128), 0)
    coord = row < 3
    centre = jnp.where(coord, jnp.broadcast_to(first[:, 0:1], (8, 128)), 0.0)
    a = first - centre
    b = second - centre
    norm_a = jnp.sum(jnp.where(coord, a * a, 0.0), axis=0, keepdims=True) + SOFT
    norm_b = jnp.sum(jnp.where(coord, b * b, 0.0), axis=0, keepdims=True)
    left = jnp.where(coord, a, jnp.where(row == 3, norm_a, jnp.where(row == 5, 1.0, 0.0)))
    right = jnp.where(coord, -2.0 * b, jnp.where(row == 3, 1.0, jnp.where(row == 5, norm_b, 0.0)))
    load = None
    if with_pressure:
        left = jnp.where(row == 4, first[3:4, :], left)
        load = jnp.where(row == 4, 1.0, jnp.where(row == 5, second[3:4, :], 0.0))
    return a, b, left, right, load


def six_left(parts):
    h, m, l = parts
    return stack([h, h, m, m, h, l])


def six_right(parts):
    h, m, l = parts
    return stack([h, m, h, m, l, h])


def tile_at(ref, slot):
    return ref[slot]


def rest_group(ks, pair_s, slots_ref, flags_ref, c1_ref, c2_ref):
    squares = []
    for k in ks:
        _, _, left, right, _ = pair_rows(
            tile_at(slots_ref, pair_s[0, k]), tile_at(slots_ref, pair_s[1, k]), False
        )
        squares.append((six_left(split(left)), six_right(split(right))))
    squares = [dot(left, right, 0, 0) for left, right in squares]
    sub = lax.broadcasted_iota(jnp.int32, (8, 128), 0)
    for k, square in zip(ks, squares):
        for t in range(16):
            w0, w1 = (8 * t) // 14, (8 * t + 7) // 14
            word = jnp.broadcast_to(flags_ref[w0, pl.ds(k, 1), :], (8, 128))
            if w1 != w0:
                other = jnp.broadcast_to(flags_ref[w1, pl.ds(k, 1), :], (8, 128))
                word = jnp.where(sub < (14 * w1 - 8 * t), word, other)
            bit = lax.shift_left(jnp.int32(1), lax.rem(sub + 8 * t, 14))
            value = jnp.maximum(square[8 * t : 8 * t + 8, :], SOFT)
            inverse = lax.rsqrt(value)
            q = lax.rsqrt(value + (REACH - SOFT))
            c2 = jnp.where(jnp.bitwise_and(word, bit) != 0, q * q, 0.0)
            c1_ref[k, pl.ds(8 * t, 8), :] = c2 * inverse
            c2_ref[k, pl.ds(8 * t, 8), :] = c2


def bond_factors(buffer, ks, pair_s, slots_ref, c1_ref, c2_ref, factor, coords, tiles):
    pre = []
    for d, k in enumerate(ks):
        a, b, left, right, load = pair_rows(
            tile_at(slots_ref, pair_s[0, k]), tile_at(slots_ref, pair_s[1, k]), True
        )
        ls, rs, ps = split(left), split(right), split(load)
        pre.append((six_left(ls), jnp.concatenate([six_right(rs), six_right(ps)], axis=1)))
        coords[buffer, d, 0] = stack(ls[:2])
        coords[buffer, d, 1] = stack(rs[:2])
        tiles[buffer, d, 0] = a
        tiles[buffer, d, 1] = b
    products = [dot(left, right, 0, 0) for left, right in pre]
    for d, (k, product) in enumerate(zip(ks, products)):
        for t in range(8):
            rows = slice(16 * t, 16 * t + 16)
            square = jnp.maximum(product[rows, :128], SOFT)
            load = product[rows, 128:]
            f = c1_ref[k, pl.ds(16 * t, 16), :] - c2_ref[k, pl.ds(16 * t, 16), :] * (
                load * lax.rsqrt(square)
            )
            high = f.astype(BF16)
            factor[buffer, d, 0, rows, :] = high
            factor[buffer, d, 1, rows, :] = (f - high.astype(F32)).astype(BF16)


def bond_sums(buffer, ks, on_ref, factor, coords, tiles):
    sums = []
    for d in range(len(ks)):
        ca, cb = coords[buffer, d, 0], coords[buffer, d, 1]
        high, low = factor[buffer, d, 0], factor[buffer, d, 1]
        sums.append(
            (
                dot(
                    jnp.concatenate([cb, cb], axis=1),
                    jnp.concatenate([high, low], axis=1), 1, 1,
                ),
                dot(jnp.concatenate([ca, ca], axis=1), stack([high, low])),
            )
        )
    for d, (k, (ga, gb)) in enumerate(zip(ks, sums)):
        ga = ga[0:8] + ga[8:16]
        gb = gb[0:8] + gb[8:16]
        on_a = -0.5 * ga - tiles[buffer, d, 0] * ga[3:4, :]
        on_b = gb - tiles[buffer, d, 1] * gb[5:6, :]
        on_ref[pl.ds(k, 3, stride=2 * PAIRS), :] = on_a[0:3]
        on_ref[pl.ds(PAIRS + k, 3, stride=2 * PAIRS), :] = on_b[0:3]


def kernel(
    pair_s, count_s, ref, disp, vel, pres, cond, mask, send_v, pair_v, flags_any,
    state,
    flags, rest, shift, speed, owner, chooser, slots_rest, slots_move, on, c1, c2,
    factor, coords, tiles,
    ref_out, ref_in, mov_out0, mov_out1, mov_in0, mov_in1, frc_out0, frc_out1, frc_in0, frc_in1,
    load_out, load_in,
    cells0, cells1, west0, east0, west1, east1, north0, south0, north1, south1,
    face_n, face_s, face_w, face_e, press, wet,
    flag_sem, send_sem, recv_sem, halo_send, halo_recv,
):
    s = lax.axis_index("slab")
    u = lax.axis_index("sub")
    slabs = lax.axis_size("slab")
    subs = lax.axis_size("sub")
    y, x = s // SIDE, s % SIDE
    odd = u % 2
    targets, sources = [], []
    for dy, dx in ORDER:
        ty = dy + odd * ((SIDE - dx) % SIDE - dy)
        tx = dx + odd * (dy - dx)
        targets.append(((y + ty) % SIDE) * SIDE + (x + tx) % SIDE)
        sources.append(((y + SIDE - ty) % SIDE) * SIDE + (x + SIDE - tx) % SIDE)
    up, down = (s + slabs - 1) % slabs, (s + 1) % slabs
    left, right = (u + subs - 1) % subs, (u + 1) % subs

    barrier = pltpu.get_barrier_semaphore()
    for target in targets:
        pl.semaphore_signal(barrier, inc=1, device_id=(target, u), device_id_type=MESH)
    for v in (left, right):
        pl.semaphore_signal(barrier, inc=1, device_id=(s, v), device_id_type=MESH)
    flag_copy = pltpu.make_async_copy(flags_any, flags, flag_sem)
    flag_copy.start()

    def gather_blocks(pairs_of_refs):
        for l in range(NB):
            for src, dst in pairs_of_refs:
                dst[pl.ds(l, 3, stride=NB), :] = src[:, 128 * l : 128 * l + 128]

    def fields(buffer):
        return [buffer[f * NB : (f + 1) * NB, :] for f in range(3)]

    def placed():
        return [r + d for r, d in zip(fields(rest), fields(shift))]

    def load_of(pressure):
        return 0.5 + (0.5 * COUPLING) * (pressure * wet[...])

    def choose(values, dst):
        parts = split(jnp.concatenate(values, axis=1))
        for row in range(SIDE):
            pick = chooser[row * SIDE * CAP : (row + 1) * SIDE * CAP, :]
            picked = dot(pick, parts[0]) + dot(pick, parts[1]) + dot(pick, parts[2])
            for q in range(SIDE):
                for f in range(len(values)):
                    dst[row * SIDE + q, f * CAP : (f + 1) * CAP, :] = picked[
                        q * CAP : (q + 1) * CAP, f * 128 : (f + 1) * 128
                    ]

    def send(src, dst, phase):
        copies = []
        for n, target in enumerate(targets):
            copy = pltpu.make_async_remote_copy(
                src_ref=src.at[target],
                dst_ref=dst.at[s],
                send_sem=send_sem.at[phase, n],
                recv_sem=recv_sem.at[phase, n],
                device_id=(target, u),
                device_id_type=MESH,
            )
            copy.start()
            copies.append(copy)
        return copies

    def place(src, dst, p, first, count):
        for f in range(count):
            for g in range(CAP // 8):
                dst[pl.ds(p * CAP + 8 * g, 8), first + f, :] = src[
                    p, pl.ds(f * CAP + 8 * g, 8), :
                ]

    def receive(copies, own, src, dst, first, count):
        place(own, dst, s, first, count)
        for copy, p in zip(copies, sources):
            copy.wait_recv()
            place(src, dst, p, first, count)

    def halo(src, n, dev, dst):
        return pltpu.make_async_remote_copy(
            src_ref=src, dst_ref=dst, send_sem=halo_send.at[n], recv_sem=halo_recv.at[n],
            device_id=dev, device_id_type=MESH,
        )

    rows = lax.broadcasted_iota(jnp.int32, (64, 128), 0)
    lanes = lax.broadcasted_iota(jnp.int32, (64, 128), 1)

    def neighbours(centre, north, south, west, east):
        return (
            jnp.where(rows == 0, north[7:8, :], pltpu.roll(centre, 1, 0)),
            jnp.where(rows == 63, south[0:1, :], pltpu.roll(centre, 63, 0)),
            jnp.where(lanes == 0, pltpu.roll(west, 1, 1), pltpu.roll(centre, 1, 1)),
            jnp.where(lanes == 127, pltpu.roll(east, 127, 1), pltpu.roll(centre, 127, 1)),
        )

    def faces():
        inside = (
            jnp.logical_or(rows > 0, s > 0),
            jnp.logical_or(rows < 63, s < slabs - 1),
            jnp.logical_or(lanes > 0, u > 0),
            jnp.logical_or(lanes < 127, u < subs - 1),
        )
        wets = neighbours(wet[...], north0[1], south0[1], west0[1], east0[1])
        rocks = neighbours(cells0[2], north0[2], south0[2], west0[2], east0[2])
        for face, ok, w, r in zip((face_n, face_s, face_w, face_e), inside, wets, rocks):
            value = 0.5 * (cond[...] * wet[...] * w + r * wet[...])
            face[...] = jnp.where(ok, value, 0.0)

    def flow(north, south, west, east):
        centre = press[...]
        total = jnp.zeros_like(centre)
        around = neighbours(centre, north, south, west, east)
        for face, value in zip((face_s, face_n, face_e, face_w), (1, 0, 3, 2)):
            total = total + face[...] * (around[value] - centre)
        press[...] = centre + FLOW * total

    def pair_forces():
        def members(j):
            return [j * GROUP + d for d in range(GROUP)]

        def make(buffer, j):
            bond_factors(buffer, members(j), pair_s, slots_move, c1, c2, factor, coords, tiles)

        def add(buffer, j):
            bond_sums(buffer, members(j), on, factor, coords, tiles)

        groups = PAIRS // GROUP
        make(0, 0)

        @pl.loop(0, groups // 2 - 1)
        def _(i):
            add(0, 2 * i)
            make(1, 2 * i + 1)
            add(1, 2 * i + 1)
            make(0, 2 * i + 2)

        add(0, groups - 2)
        make(1, groups - 1)
        add(1, groups - 1)

    def give_back(src, dst, phase):
        live = lax.broadcasted_iota(jnp.int32, (2, PAIRS), 1) < count_s[0]
        named = jnp.where(live, pair_v[...], -1)
        ends = jnp.concatenate([named[0:1, :], named[1:2, :]], axis=1)
        parts = split(
            jnp.concatenate([on[f * 2 * PAIRS : (f + 1) * 2 * PAIRS, :] for f in range(3)], axis=1)
        )
        for row in range(SIDE):
            slot = lax.broadcasted_iota(jnp.int32, (SIDE * CAP, 2 * PAIRS), 0) + row * (SIDE * CAP)
            hit = jnp.where(slot == ends, 1.0, 0.0).astype(BF16)
            total = dot(hit, parts[0]) + dot(hit, parts[1])
            for q in range(SIDE):
                for f in range(3):
                    src[row * SIDE + q, f * CAP : (f + 1) * CAP, :] = total[
                        q * CAP : (q + 1) * CAP, f * 128 : (f + 1) * 128
                    ]
        copies = send(src, dst, phase)
        dst[s] = src[s]
        return copies

    def advance(frc_in):
        parts = split(
            jnp.concatenate(
                [
                    frc_in[:, f * CAP : (f + 1) * CAP, :].reshape(PEERS * CAP, 128)
                    for f in range(3)
                ],
                axis=1,
            )
        )
        table = owner[...]
        force = dot(table, parts[0]) + dot(table, parts[1])
        for f in range(3):
            part = slice(f * NB, (f + 1) * NB)
            v = speed[part, :] + (DT * FORCE_SCALE) * force[:, f * 128 : (f + 1) * 128]
            speed[part, :] = v
            shift[part, :] = shift[part, :] + DT * v

    gather_blocks([(ref, rest)])
    chosen = jnp.concatenate([send_v[p : p + 1, :] for p in range(PEERS)], axis=1)
    block = lax.broadcasted_iota(jnp.int32, (NB, PEERS * CAP), 0)
    table = jnp.where(chosen == block, 1.0, 0.0)
    owner[...] = table.astype(BF16)
    chooser[...] = jnp.transpose(table).astype(BF16)
    choose(fields(rest), ref_out)
    pl.semaphore_wait(barrier, len(ORDER) + 2)
    rest_copies = send(ref_out, ref_in, 0)

    gather_blocks([(disp, shift), (vel, speed)])
    wet[...] = mask[...].astype(F32)
    press[...] = pres[...]
    choose(placed() + [load_of(press[...])], mov_out0)
    cells0[0] = pres[...]
    cells0[1] = wet[...]
    cells0[2] = cond[...] * wet[...]
    for copy in rest_copies:
        copy.wait_send()
    move_copies = send(mov_out0, mov_in0, 1)
    halos = [
        halo(cells0.at[:, pl.ds(56, 8)], 0, (down, u), north0),
        halo(cells0.at[:, pl.ds(0, 8)], 1, (up, u), south0),
        halo(cells0, 2, (s, right), west0),
        halo(cells0, 3, (s, left), east0),
    ]
    for copy in halos:
        copy.start()
    slots_rest[...] = jnp.zeros_like(slots_rest)
    slots_move[...] = jnp.zeros_like(slots_move)

    receive(rest_copies, ref_out, ref_in, slots_rest, 0, 3)
    flag_copy.wait()

    @pl.loop(0, PAIRS // REST_GROUP)
    def _(j):
        rest_group(
            [j * REST_GROUP + d for d in range(REST_GROUP)], pair_s, slots_rest, flags, c1, c2
        )

    for copy in halos:
        copy.wait_recv()
    faces()
    flow(north0[0], south0[0], west0[0], east0[0])
    choose([load_of(press[...])], load_out)
    receive(move_copies, mov_out0, mov_in0, slots_move, 0, 4)
    load_copies = send(load_out, load_in, 3)
    cells1[...] = press[...]
    halos1 = [
        halo(cells1.at[pl.ds(56, 8)], 4, (down, u), north1),
        halo(cells1.at[pl.ds(0, 8)], 5, (up, u), south1),
        halo(cells1, 6, (s, right), west1),
        halo(cells1, 7, (s, left), east1),
    ]
    for copy in halos1:
        copy.start()

    pair_forces()
    back_copies = give_back(frc_out0, frc_in0, 2)
    receive(load_copies, load_out, load_in, slots_move, 3, 1)
    for copy in halos1:
        copy.wait_recv()
    flow(north1[...], south1[...], west1[...], east1[...])
    state[6 * NB :, :] = press[...]
    for copy in back_copies:
        copy.wait_recv()
    advance(frc_in0)

    choose(placed(), mov_out1)
    next_copies = send(mov_out1, mov_in1, 4)
    receive(next_copies, mov_out1, mov_in1, slots_move, 0, 3)
    pair_forces()
    last_copies = give_back(frc_out1, frc_in1, 5)
    for copy in last_copies:
        copy.wait_recv()
    advance(frc_in1)
    state[0 : 3 * NB, :] = shift[...]
    state[3 * NB : 6 * NB, :] = speed[...]
    for copies in (move_copies, halos, load_copies, halos1, back_copies, next_copies, last_copies):
        for copy in copies:
            copy.wait_send()


def unpack_kernel(state, disp_o, vel_o, pres_o):
    for l in range(NB):
        lanes = slice(128 * l, 128 * l + 128)
        disp_o[:, lanes] = state[pl.ds(l, 3, stride=NB), :]
        vel_o[:, lanes] = state[pl.ds(3 * NB + l, 3, stride=NB), :]
    pres_o[...] = state[6 * NB :, :]


def body(ref_pos, disp, vel, pressure, conductivity, frac_mask, send_list, pair_list, pair_count, bond_flags):
    vmem = pl.BlockSpec(memory_space=pltpu.VMEM)
    smem = pl.BlockSpec(memory_space=pltpu.SMEM)
    pairs = pair_list.T
    grid = pltpu.VMEM((64, 128), F32)
    three = pltpu.VMEM((3 * NB, 128), F32)
    third = pltpu.VMEM((PEERS, 3 * CAP, 128), F32)
    first = pltpu.VMEM((PEERS, CAP, 128), F32)
    fourth = pltpu.VMEM((PEERS, 4 * CAP, 128), F32)
    slots = pltpu.VMEM((PEERS * CAP, 8, 128), F32)
    grids = pltpu.VMEM((3, 64, 128), F32)
    strips = pltpu.VMEM((3, 8, 128), F32)
    strip = pltpu.VMEM((8, 128), F32)
    bonds = pltpu.VMEM((PAIRS, 128, 128), F32)
    state = pl.pallas_call(
        kernel,
        out_shape=jax.ShapeDtypeStruct((7 * NB, 128), F32),
        in_specs=[smem, smem] + [vmem] * 8 + [pl.BlockSpec(memory_space=pl.ANY)],
        out_specs=vmem,
        scratch_shapes=[
            pltpu.VMEM((10, PAIRS, 128), jnp.int32),
            three, three, three,
            pltpu.VMEM((NB, PEERS * CAP), BF16),
            pltpu.VMEM((PEERS * CAP, NB), BF16),
            slots, slots,
            pltpu.VMEM((3 * 2 * PAIRS, 128), F32),
            bonds, bonds,
            pltpu.VMEM((2, GROUP, 2, 128, 128), BF16),
            pltpu.VMEM((2, GROUP, 2, 16, 128), BF16),
            pltpu.VMEM((2, GROUP, 2, 8, 128), F32),
            third, third, fourth, third, fourth, third, third, third, third, third, first, first,
            grids, grid, grids, grids, grid, grid, strips, strips, strip, strip,
            grid, grid, grid, grid, grid, grid,
            pltpu.SemaphoreType.DMA,
            pltpu.SemaphoreType.DMA((6, PEERS)),
            pltpu.SemaphoreType.DMA((6, PEERS)),
            pltpu.SemaphoreType.DMA((8,)),
            pltpu.SemaphoreType.DMA((8,)),
        ],
        compiler_params=pltpu.CompilerParams(
            collective_id=0, has_side_effects=True, vmem_limit_bytes=58 << 20
        ),
    )(
        pairs, pair_count, ref_pos, disp, vel, pressure, conductivity, frac_mask, send_list, pairs,
        bond_flags.transpose(1, 0, 2),
    )
    return pl.pallas_call(
        unpack_kernel,
        out_shape=(
            jax.ShapeDtypeStruct(disp.shape, F32),
            jax.ShapeDtypeStruct(vel.shape, F32),
            jax.ShapeDtypeStruct(pressure.shape, F32),
        ),
        in_specs=[vmem],
        out_specs=(vmem, vmem, vmem),
    )(state)


def solution(mesh):
    in_specs = (
        P(None, ("slab", "sub")),
        P(None, ("slab", "sub")),
        P(None, ("slab", "sub")),
        P("slab", "sub"),
        P("slab", "sub"),
        P("slab", "sub"),
        P(("slab", "sub"), None),
        P(("slab", "sub"), None),
        P(("slab", "sub")),
        P(("slab", "sub"), None, None),
    )
    out_specs = (P(None, ("slab", "sub")), P(None, ("slab", "sub")), P("slab", "sub"))
    return jax.shard_map(body, mesh=mesh, in_specs=in_specs, out_specs=out_specs, check_vma=False)
```

```python
import functools

import jax
import jax.numpy as jnp
from jax import lax
from jax.experimental import pallas as pl
from jax.experimental.pallas import tpu as pltpu
from jax.sharding import PartitionSpec as P

MESH = pl.DeviceIdType.MESH
F32 = jnp.float32
BF16 = jnp.bfloat16

STEPS = 2
SOFT = 0.0025
REACH = 0.09
COUPLING = 0.3
DT = 0.2
FORCE_SCALE = 4.0 * REACH
FLOW = 1.0

NB = 64
CAP = 32
PAIRS = 256
SIDE = 4
PEERS = SIDE * SIDE
GROUP = 16
REST_GROUP = 16
NEAR = 8
ORDER = [
    (0, 1), (1, 0), (0, 3), (3, 0), (1, 1), (3, 3), (1, 3), (3, 1),
    (0, 2), (2, 0), (1, 2), (2, 1), (3, 2), (2, 3), (2, 2),
]


def dot(a, b, ca=1, cb=0):
    return lax.dot_general(a, b, (((ca,), (cb,)), ((), ())), preferred_element_type=F32)


def split(t):
    high = t.astype(BF16)
    rest = t - high.astype(F32)
    mid = rest.astype(BF16)
    low = (rest - mid.astype(F32)).astype(BF16)
    return high, mid, low


def stack(parts):
    return jnp.concatenate(parts, axis=0)


def pair_rows(first, second, with_pressure):
    row = lax.broadcasted_iota(jnp.int32, (8, 128), 0)
    coord = row < 3
    centre = jnp.where(coord, jnp.broadcast_to(first[:, 0:1], (8, 128)), 0.0)
    a = first - centre
    b = second - centre
    norm_a = jnp.sum(jnp.where(coord, a * a, 0.0), axis=0, keepdims=True) + SOFT
    norm_b = jnp.sum(jnp.where(coord, b * b, 0.0), axis=0, keepdims=True)
    left = jnp.where(coord, a, jnp.where(row == 3, norm_a, jnp.where(row == 5, 1.0, 0.0)))
    right = jnp.where(coord, -2.0 * b, jnp.where(row == 3, 1.0, jnp.where(row == 5, norm_b, 0.0)))
    load = None
    if with_pressure:
        left = jnp.where(row == 4, first[3:4, :], left)
        load = jnp.where(row == 4, 1.0, jnp.where(row == 5, second[3:4, :], 0.0))
    return a, b, left, right, load


def six_left(parts):
    h, m, l = parts
    return stack([h, h, m, m, h, l])


def six_right(parts):
    h, m, l = parts
    return stack([h, m, h, m, l, h])


def tile_at(ref, slot):
    return ref[slot]


def rest_group(ks, pair_s, slots_ref, flags_ref, c1_ref, c2_ref):
    squares = []
    for k in ks:
        _, _, left, right, _ = pair_rows(
            tile_at(slots_ref, pair_s[0, k]), tile_at(slots_ref, pair_s[1, k]), False
        )
        squares.append((six_left(split(left)), six_right(split(right))))
    squares = [dot(left, right, 0, 0) for left, right in squares]
    sub = lax.broadcasted_iota(jnp.int32, (8, 128), 0)
    for k, square in zip(ks, squares):
        for t in range(16):
            w0, w1 = (8 * t) // 14, (8 * t + 7) // 14
            word = jnp.broadcast_to(flags_ref[w0, pl.ds(k, 1), :], (8, 128))
            if w1 != w0:
                other = jnp.broadcast_to(flags_ref[w1, pl.ds(k, 1), :], (8, 128))
                word = jnp.where(sub < (14 * w1 - 8 * t), word, other)
            bit = lax.shift_left(jnp.int32(1), lax.rem(sub + 8 * t, 14))
            value = jnp.maximum(square[8 * t : 8 * t + 8, :], SOFT)
            inverse = lax.rsqrt(value)
            q = lax.rsqrt(value + (REACH - SOFT))
            c2 = jnp.where(jnp.bitwise_and(word, bit) != 0, q * q, 0.0)
            c1_ref[k, pl.ds(8 * t, 8), :] = c2 * inverse
            c2_ref[k, pl.ds(8 * t, 8), :] = c2


def bond_factors(buffer, ks, pair_s, slots_ref, c1_ref, c2_ref, factor, coords, tiles):
    pre = []
    for d, k in enumerate(ks):
        a, b, left, right, load = pair_rows(
            tile_at(slots_ref, pair_s[0, k]), tile_at(slots_ref, pair_s[1, k]), True
        )
        ls, rs, ps = split(left), split(right), split(load)
        pre.append((six_left(ls), jnp.concatenate([six_right(rs), six_right(ps)], axis=1)))
        coords[buffer, d, 0] = stack(ls[:2])
        coords[buffer, d, 1] = stack(rs[:2])
        tiles[buffer, d, 0] = a
        tiles[buffer, d, 1] = b
    products = [dot(left, right, 0, 0) for left, right in pre]
    for d, (k, product) in enumerate(zip(ks, products)):
        for t in range(8):
            rows = slice(16 * t, 16 * t + 16)
            square = jnp.maximum(product[rows, :128], SOFT)
            load = product[rows, 128:]
            f = c1_ref[k, pl.ds(16 * t, 16), :] - c2_ref[k, pl.ds(16 * t, 16), :] * (
                load * lax.rsqrt(square)
            )
            high = f.astype(BF16)
            factor[buffer, d, 0, rows, :] = high
            factor[buffer, d, 1, rows, :] = (f - high.astype(F32)).astype(BF16)


def bond_sums(buffer, ks, on_ref, factor, coords, tiles):
    sums = []
    for d in range(len(ks)):
        ca, cb = coords[buffer, d, 0], coords[buffer, d, 1]
        high, low = factor[buffer, d, 0], factor[buffer, d, 1]
        wide = jnp.concatenate([high, low], axis=1)
        on_first = dot(wide, jnp.concatenate([cb, cb], axis=1), 1, 1)
        on_second = dot(ca, wide)
        sums.append((jnp.transpose(on_first), on_second[:, :128] + on_second[:, 128:]))
    for d, (k, (ga, gb)) in enumerate(zip(ks, sums)):
        ga = ga[0:8] + ga[8:16]
        gb = gb[0:8] + gb[8:16]
        on_a = -0.5 * ga - tiles[buffer, d, 0] * ga[3:4, :]
        on_b = gb - tiles[buffer, d, 1] * gb[5:6, :]
        on_ref[pl.ds(k, 3, stride=2 * PAIRS), :] = on_a[0:3]
        on_ref[pl.ds(PAIRS + k, 3, stride=2 * PAIRS), :] = on_b[0:3]


def kernel(
    pair_s, count_s, ref_any, disp_any, vel_any, pres_any, cond_any, mask_any, send_any, pair_any, flags_any,
    state,
    ref, disp, vel, pres, cond, mask, send_v, pair_v, flags, rest, shift, speed, chooser, slots_rest, slots_move, on, c1, c2,
    factor, coords, tiles,
    ref_out, ref_in, mov_out0, mov_out1, mov_in0, mov_in1, frc_out0, frc_out1, frc_in0, frc_in1,
    load_out, load_in,
    cells0, cells1, west0, east0, west1, east1, north0, south0, north1, south1,
    face_n, face_s, face_w, face_e, press, wet,
    in_sem, send_sem, recv_sem, halo_send, halo_recv,
):
    s = lax.axis_index("slab")
    u = lax.axis_index("sub")
    slabs = lax.axis_size("slab")
    subs = lax.axis_size("sub")
    y, x = s // SIDE, s % SIDE
    odd = u % 2
    targets, sources = [], []
    for dy, dx in ORDER:
        ty = dy + odd * ((SIDE - dx) % SIDE - dy)
        tx = dx + odd * (dy - dx)
        targets.append(((y + ty) % SIDE) * SIDE + (x + tx) % SIDE)
        sources.append(((y + SIDE - ty) % SIDE) * SIDE + (x + SIDE - tx) % SIDE)
    up, down = (s + slabs - 1) % slabs, (s + 1) % slabs
    left, right = (u + subs - 1) % subs, (u + 1) % subs

    loads = []
    for n, (src, dst) in enumerate(
        (
            (send_any, send_v), (ref_any, ref), (disp_any, disp), (vel_any, vel), (pres_any, pres),
            (mask_any, mask), (cond_any, cond), (pair_any, pair_v), (flags_any, flags),
        )
    ):
        loads.append(pltpu.make_async_copy(src, dst, in_sem.at[n]))
        loads[n].start()

    barrier = pltpu.get_barrier_semaphore()
    for target in targets:
        pl.semaphore_signal(barrier, inc=1, device_id=(target, u), device_id_type=MESH)
    for v in (left, right):
        pl.semaphore_signal(barrier, inc=1, device_id=(s, v), device_id_type=MESH)

    def gather_blocks(pairs_of_refs):
        for l in range(NB):
            for src, dst in pairs_of_refs:
                dst[pl.ds(l, 3, stride=NB), :] = src[:, 128 * l : 128 * l + 128]

    def fields(buffer):
        return [buffer[f * NB : (f + 1) * NB, :] for f in range(3)]

    def placed():
        return [r + d for r, d in zip(fields(rest), fields(shift))]

    def load_of(pressure):
        return 0.5 + (0.5 * COUPLING) * (pressure * wet[...])

    def start(src, dst, phase, part):
        copies = []
        for n in part:
            copy = pltpu.make_async_remote_copy(
                src_ref=src.at[targets[n]],
                dst_ref=dst.at[s],
                send_sem=send_sem.at[phase, n],
                recv_sem=recv_sem.at[phase, n],
                device_id=(targets[n], u),
                device_id_type=MESH,
            )
            copy.start()
            copies.append(copy)
        return copies

    def fill(row, picked, dst, count):
        for q in range(SIDE):
            for f in range(count):
                dst[row * SIDE + q, f * CAP : (f + 1) * CAP, :] = picked[
                    q * CAP : (q + 1) * CAP, f * 128 : (f + 1) * 128
                ]

    def by_rows(make_row, src, dst, phase, count, ready=None):
        copies = []
        for step in (0, 1, 3, 2):
            row = (y + step) % SIDE
            fill(row, make_row(row), src, count)
            if step == 3:
                if ready is not None:
                    ready()
                copies += start(src, dst, phase, range(NEAR))
        return copies + start(src, dst, phase, range(NEAR, len(ORDER)))

    def chosen_rows(values):
        parts = split(jnp.concatenate(values, axis=1))

        def make_row(row):
            pick = chooser[pl.ds(pl.multiple_of(row * SIDE * CAP, SIDE * CAP), SIDE * CAP), :]
            return dot(pick, parts[0]) + dot(pick, parts[1]) + dot(pick, parts[2])

        return make_row

    def place(src, dst, p, first, count):
        for f in range(count):
            for g in range(CAP // 8):
                dst[pl.ds(p * CAP + 8 * g, 8), first + f, :] = src[
                    p, pl.ds(f * CAP + 8 * g, 8), :
                ]

    def receive(copies, own, src, dst, first, count):
        place(own, dst, s, first, count)
        for copy, p in zip(copies, sources):
            copy.wait_recv()
            place(src, dst, p, first, count)

    def halo(src, n, dev, dst):
        return pltpu.make_async_remote_copy(
            src_ref=src, dst_ref=dst, send_sem=halo_send.at[n], recv_sem=halo_recv.at[n],
            device_id=dev, device_id_type=MESH,
        )

    rows = lax.broadcasted_iota(jnp.int32, (64, 128), 0)
    lanes = lax.broadcasted_iota(jnp.int32, (64, 128), 1)

    def neighbours(centre, north, south, west, east):
        return (
            jnp.where(rows == 0, north[7:8, :], pltpu.roll(centre, 1, 0)),
            jnp.where(rows == 63, south[0:1, :], pltpu.roll(centre, 63, 0)),
            jnp.where(lanes == 0, pltpu.roll(west, 1, 1), pltpu.roll(centre, 1, 1)),
            jnp.where(lanes == 127, pltpu.roll(east, 127, 1), pltpu.roll(centre, 127, 1)),
        )

    def faces():
        inside = (
            jnp.logical_or(rows > 0, s > 0),
            jnp.logical_or(rows < 63, s < slabs - 1),
            jnp.logical_or(lanes > 0, u > 0),
            jnp.logical_or(lanes < 127, u < subs - 1),
        )
        wets = neighbours(wet[...], north0[1], south0[1], west0[1], east0[1])
        rocks = neighbours(cells0[2], north0[2], south0[2], west0[2], east0[2])
        for face, ok, w, r in zip((face_n, face_s, face_w, face_e), inside, wets, rocks):
            value = 0.5 * (cond[...] * wet[...] * w + r * wet[...])
            face[...] = jnp.where(ok, value, 0.0)

    def flow(north, south, west, east):
        centre = press[...]
        total = jnp.zeros_like(centre)
        around = neighbours(centre, north, south, west, east)
        for face, value in zip((face_s, face_n, face_e, face_w), (1, 0, 3, 2)):
            total = total + face[...] * (around[value] - centre)
        press[...] = centre + FLOW * total

    def pair_forces():
        def members(j):
            return [j * GROUP + d for d in range(GROUP)]

        def make(buffer, j):
            bond_factors(buffer, members(j), pair_s, slots_move, c1, c2, factor, coords, tiles)

        def add(buffer, j):
            bond_sums(buffer, members(j), on, factor, coords, tiles)

        groups = PAIRS // GROUP
        make(0, 0)

        @pl.loop(0, groups // 2 - 1)
        def _(i):
            add(0, 2 * i)
            make(1, 2 * i + 1)
            add(1, 2 * i + 1)
            make(0, 2 * i + 2)

        add(0, groups - 2)
        make(1, groups - 1)
        add(1, groups - 1)

    def give_back(src, dst, phase):
        live = lax.broadcasted_iota(jnp.int32, (2, PAIRS), 1) < count_s[0]
        named = jnp.where(live, pair_v[...], -1)
        ends = jnp.concatenate([named[0:1, :], named[1:2, :]], axis=1)
        parts = split(
            jnp.concatenate([on[f * 2 * PAIRS : (f + 1) * 2 * PAIRS, :] for f in range(3)], axis=1)
        )

        def make_row(row):
            slot = lax.broadcasted_iota(jnp.int32, (SIDE * CAP, 2 * PAIRS), 0) + row * (SIDE * CAP)
            hit = jnp.where(slot == ends, 1.0, 0.0).astype(BF16)
            return dot(hit, parts[0]) + dot(hit, parts[1])

        return by_rows(make_row, src, dst, phase, 3)

    def force_from(src, p):
        parts = split(jnp.concatenate([src[p, f * CAP : (f + 1) * CAP, :] for f in range(3)], axis=1))
        pick = chooser[pl.ds(pl.multiple_of(p * CAP, CAP), CAP), :]
        return dot(pick, parts[0], 0, 0) + dot(pick, parts[1], 0, 0)

    def advance(copies, own, src):
        force = force_from(own, s)
        for copy, p in zip(copies, sources):
            copy.wait_recv()
            force = force + force_from(src, p)
        for f in range(3):
            part = slice(f * NB, (f + 1) * NB)
            v = speed[part, :] + (DT * FORCE_SCALE) * force[:, f * 128 : (f + 1) * 128]
            speed[part, :] = v
            shift[part, :] = shift[part, :] + DT * v

    for copy in loads[:2]:
        copy.wait()
    gather_blocks([(ref, rest)])
    chosen = jnp.concatenate([send_v[p : p + 1, :] for p in range(PEERS)], axis=1)
    block = lax.broadcasted_iota(jnp.int32, (NB, PEERS * CAP), 0)
    table = jnp.where(chosen == block, 1.0, 0.0)
    chooser[...] = jnp.transpose(table).astype(BF16)
    rest_copies = by_rows(
        chosen_rows(fields(rest)), ref_out, ref_in, 0, 3,
        lambda: pl.semaphore_wait(barrier, len(ORDER) + 2),
    )

    for copy in loads[2:7]:
        copy.wait()
    gather_blocks([(disp, shift), (vel, speed)])
    wet[...] = mask[...].astype(F32)
    press[...] = pres[...]
    make_row = chosen_rows(placed() + [load_of(press[...])])
    for row in range(SIDE):
        fill(row, make_row(row), mov_out0, 4)
    cells0[0] = pres[...]
    cells0[1] = wet[...]
    cells0[2] = cond[...] * wet[...]
    for copy in rest_copies:
        copy.wait_send()
    move_copies = start(mov_out0, mov_in0, 1, range(len(ORDER)))
    halos = [
        halo(cells0.at[:, pl.ds(56, 8)], 0, (down, u), north0),
        halo(cells0.at[:, pl.ds(0, 8)], 1, (up, u), south0),
        halo(cells0, 2, (s, right), west0),
        halo(cells0, 3, (s, left), east0),
    ]
    for copy in halos:
        copy.start()
    slots_rest[...] = jnp.zeros_like(slots_rest)
    slots_move[...] = jnp.zeros_like(slots_move)

    receive(rest_copies, ref_out, ref_in, slots_rest, 0, 3)
    for copy in loads[7:]:
        copy.wait()

    @pl.loop(0, PAIRS // REST_GROUP)
    def _(j):
        rest_group(
            [j * REST_GROUP + d for d in range(REST_GROUP)], pair_s, slots_rest, flags, c1, c2
        )

    for copy in halos:
        copy.wait_recv()
    faces()
    flow(north0[0], south0[0], west0[0], east0[0])
    make_row = chosen_rows([load_of(press[...])])
    for row in range(SIDE):
        fill(row, make_row(row), load_out, 1)
    receive(move_copies, mov_out0, mov_in0, slots_move, 0, 4)
    load_copies = start(load_out, load_in, 3, range(len(ORDER)))
    cells1[...] = press[...]
    halos1 = [
        halo(cells1.at[pl.ds(56, 8)], 4, (down, u), north1),
        halo(cells1.at[pl.ds(0, 8)], 5, (up, u), south1),
        halo(cells1, 6, (s, right), west1),
        halo(cells1, 7, (s, left), east1),
    ]
    for copy in halos1:
        copy.start()

    pair_forces()
    back_copies = give_back(frc_out0, frc_in0, 2)
    receive(load_copies, load_out, load_in, slots_move, 3, 1)
    for copy in halos1:
        copy.wait_recv()
    flow(north1[...], south1[...], west1[...], east1[...])
    state[6 * NB :, :] = press[...]
    advance(back_copies, frc_out0, frc_in0)

    next_copies = by_rows(chosen_rows(placed()), mov_out1, mov_in1, 4, 3)
    receive(next_copies, mov_out1, mov_in1, slots_move, 0, 3)
    pair_forces()
    last_copies = give_back(frc_out1, frc_in1, 5)
    advance(last_copies, frc_out1, frc_in1)
    state[0 : 3 * NB, :] = shift[...]
    state[3 * NB : 6 * NB, :] = speed[...]
    for copies in (move_copies, halos, load_copies, halos1, back_copies, next_copies, last_copies):
        for copy in copies:
            copy.wait_send()


def unpack_kernel(state, disp_o, vel_o, pres_o):
    for l in range(NB):
        lanes = slice(128 * l, 128 * l + 128)
        disp_o[:, lanes] = state[pl.ds(l, 3, stride=NB), :]
        vel_o[:, lanes] = state[pl.ds(3 * NB + l, 3, stride=NB), :]
    pres_o[...] = state[6 * NB :, :]


def body(ref_pos, disp, vel, pressure, conductivity, frac_mask, send_list, pair_list, pair_count, bond_flags):
    vmem = pl.BlockSpec(memory_space=pltpu.VMEM)
    smem = pl.BlockSpec(memory_space=pltpu.SMEM)
    pairs = pair_list.T
    grid = pltpu.VMEM((64, 128), F32)
    whole = pltpu.VMEM((64, 128), jnp.int32)
    wide = pltpu.VMEM((3, NB * 128), F32)
    three = pltpu.VMEM((3 * NB, 128), F32)
    third = pltpu.VMEM((PEERS, 3 * CAP, 128), F32)
    first = pltpu.VMEM((PEERS, CAP, 128), F32)
    fourth = pltpu.VMEM((PEERS, 4 * CAP, 128), F32)
    slots = pltpu.VMEM((PEERS * CAP, 8, 128), F32)
    grids = pltpu.VMEM((3, 64, 128), F32)
    strips = pltpu.VMEM((3, 8, 128), F32)
    strip = pltpu.VMEM((8, 128), F32)
    bonds = pltpu.VMEM((PAIRS, 128, 128), F32)
    state = pl.pallas_call(
        kernel,
        out_shape=jax.ShapeDtypeStruct((7 * NB, 128), F32),
        in_specs=[smem, smem] + [pl.BlockSpec(memory_space=pl.ANY)] * 9,
        out_specs=vmem,
        scratch_shapes=[
            wide, wide, wide, grid, grid, whole, pltpu.VMEM((PEERS, CAP), jnp.int32), pltpu.VMEM((2, PAIRS), jnp.int32),
            pltpu.VMEM((10, PAIRS, 128), jnp.int32),
            three, three, three,
            pltpu.VMEM((PEERS * CAP, NB), BF16),
            slots, slots,
            pltpu.VMEM((3 * 2 * PAIRS, 128), F32),
            bonds, bonds,
            pltpu.VMEM((2, GROUP, 2, 128, 128), BF16),
            pltpu.VMEM((2, GROUP, 2, 16, 128), BF16),
            pltpu.VMEM((2, GROUP, 2, 8, 128), F32),
            third, third, fourth, third, fourth, third, third, third, third, third, first, first,
            grids, grid, grids, grids, grid, grid, strips, strips, strip, strip,
            grid, grid, grid, grid, grid, grid,
            pltpu.SemaphoreType.DMA((9,)),
            pltpu.SemaphoreType.DMA((6, PEERS)),
            pltpu.SemaphoreType.DMA((6, PEERS)),
            pltpu.SemaphoreType.DMA((8,)),
            pltpu.SemaphoreType.DMA((8,)),
        ],
        compiler_params=pltpu.CompilerParams(
            collective_id=0, has_side_effects=True, vmem_limit_bytes=58 << 20
        ),
    )(
        pairs, pair_count, ref_pos, disp, vel, pressure, conductivity, frac_mask, send_list, pairs,
        bond_flags.transpose(1, 0, 2),
    )
    return pl.pallas_call(
        unpack_kernel,
        out_shape=(
            jax.ShapeDtypeStruct(disp.shape, F32),
            jax.ShapeDtypeStruct(vel.shape, F32),
            jax.ShapeDtypeStruct(pressure.shape, F32),
        ),
        in_specs=[vmem],
        out_specs=(vmem, vmem, vmem),
    )(state)


def solution(mesh):
    in_specs = (
        P(None, ("slab", "sub")),
        P(None, ("slab", "sub")),
        P(None, ("slab", "sub")),
        P("slab", "sub"),
        P("slab", "sub"),
        P("slab", "sub"),
        P(("slab", "sub"), None),
        P(("slab", "sub"), None),
        P(("slab", "sub")),
        P(("slab", "sub"), None, None),
    )
    out_specs = (P(None, ("slab", "sub")), P(None, ("slab", "sub")), P("slab", "sub"))
    return jax.shard_map(body, mesh=mesh, in_specs=in_specs, out_specs=out_specs, check_vma=False)
```

```python
import functools

import jax
import jax.numpy as jnp
from jax import lax
from jax.experimental import pallas as pl
from jax.experimental.pallas import tpu as pltpu
from jax.sharding import PartitionSpec as P

MESH = pl.DeviceIdType.MESH
F32 = jnp.float32
BF16 = jnp.bfloat16

STEPS = 2
SOFT = 0.0025
REACH = 0.09
COUPLING = 0.3
DT = 0.2
FORCE_SCALE = 4.0 * REACH
FLOW = 1.0

NB = 64
CAP = 32
PAIRS = 256
SIDE = 4
PEERS = SIDE * SIDE
GROUP = 16
REST_GROUP = 16
NEAR = 8
ORDER = [
    (0, 1), (1, 0), (0, 3), (3, 0), (1, 1), (3, 3), (1, 3), (3, 1),
    (0, 2), (2, 0), (1, 2), (2, 1), (3, 2), (2, 3), (2, 2),
]


def dot(a, b, ca=1, cb=0):
    return lax.dot_general(a, b, (((ca,), (cb,)), ((), ())), preferred_element_type=F32)


def split(t):
    high = t.astype(BF16)
    rest = t - high.astype(F32)
    mid = rest.astype(BF16)
    low = (rest - mid.astype(F32)).astype(BF16)
    return high, mid, low


def stack(parts):
    return jnp.concatenate(parts, axis=0)


def pair_rows(first, second, with_pressure):
    row = lax.broadcasted_iota(jnp.int32, (8, 128), 0)
    coord = row < 3
    centre = jnp.where(coord, jnp.broadcast_to(first[:, 0:1], (8, 128)), 0.0)
    a = first - centre
    b = second - centre
    norm_a = jnp.sum(jnp.where(coord, a * a, 0.0), axis=0, keepdims=True) + SOFT
    norm_b = jnp.sum(jnp.where(coord, b * b, 0.0), axis=0, keepdims=True)
    left = jnp.where(coord, a, jnp.where(row == 3, norm_a, jnp.where(row == 5, 1.0, 0.0)))
    right = jnp.where(coord, -2.0 * b, jnp.where(row == 3, 1.0, jnp.where(row == 5, norm_b, 0.0)))
    load = None
    if with_pressure:
        left = jnp.where(row == 4, first[3:4, :], left)
        load = jnp.where(row == 4, 1.0, jnp.where(row == 5, second[3:4, :], 0.0))
    return a, b, left, right, load


def six_left(parts):
    h, m, l = parts
    return stack([h, h, m, m, h, l])


def six_right(parts):
    h, m, l = parts
    return stack([h, m, h, m, l, h])


def tile_at(ref, slot):
    return ref[slot]


def rest_group(ks, pair_s, slots_ref, flags_ref, c1_ref, c2_ref):
    squares = []
    for k in ks:
        _, _, left, right, _ = pair_rows(
            tile_at(slots_ref, pair_s[0, k]), tile_at(slots_ref, pair_s[1, k]), False
        )
        squares.append((six_left(split(left)), six_right(split(right))))
    squares = [dot(left, right, 0, 0) for left, right in squares]
    sub = lax.broadcasted_iota(jnp.int32, (8, 128), 0)
    for k, square in zip(ks, squares):
        for t in range(16):
            w0, w1 = (8 * t) // 14, (8 * t + 7) // 14
            word = jnp.broadcast_to(flags_ref[w0, pl.ds(k, 1), :], (8, 128))
            if w1 != w0:
                other = jnp.broadcast_to(flags_ref[w1, pl.ds(k, 1), :], (8, 128))
                word = jnp.where(sub < (14 * w1 - 8 * t), word, other)
            bit = lax.shift_left(jnp.int32(1), lax.rem(sub + 8 * t, 14))
            value = jnp.maximum(square[8 * t : 8 * t + 8, :], SOFT)
            inverse = lax.rsqrt(value)
            q = lax.rsqrt(value + (REACH - SOFT))
            c2 = jnp.where(jnp.bitwise_and(word, bit) != 0, q * q, 0.0)
            c1_ref[k, pl.ds(8 * t, 8), :] = c2 * inverse
            c2_ref[k, pl.ds(8 * t, 8), :] = c2


def bond_factors(buffer, ks, pair_s, slots_ref, c1_ref, c2_ref, factor, coords, tiles):
    pre = []
    for d, k in enumerate(ks):
        a, b, left, right, load = pair_rows(
            tile_at(slots_ref, pair_s[0, k]), tile_at(slots_ref, pair_s[1, k]), True
        )
        ls, rs, ps = split(left), split(right), split(load)
        pre.append((six_left(ls), jnp.concatenate([six_right(rs), six_right(ps)], axis=1)))
        coords[buffer, d, 0] = stack(ls[:2])
        coords[buffer, d, 1] = stack(rs[:2])
        tiles[buffer, d, 0] = a
        tiles[buffer, d, 1] = b
    products = [dot(left, right, 0, 0) for left, right in pre]
    for d, (k, product) in enumerate(zip(ks, products)):
        for t in range(8):
            rows = slice(16 * t, 16 * t + 16)
            square = jnp.maximum(product[rows, :128], SOFT)
            load = product[rows, 128:]
            f = c1_ref[k, pl.ds(16 * t, 16), :] - c2_ref[k, pl.ds(16 * t, 16), :] * (
                load * lax.rsqrt(square)
            )
            high = f.astype(BF16)
            factor[buffer, d, 0, rows, :] = high
            factor[buffer, d, 1, rows, :] = (f - high.astype(F32)).astype(BF16)


def bond_sums(buffer, ks, on_ref, factor, coords, tiles):
    sums = []
    for d in range(len(ks)):
        ca, cb = coords[buffer, d, 0], coords[buffer, d, 1]
        high, low = factor[buffer, d, 0], factor[buffer, d, 1]
        wide = jnp.concatenate([high, low], axis=1)
        on_first = dot(wide, jnp.concatenate([cb, cb], axis=1), 1, 1)
        on_second = dot(ca, wide)
        sums.append((jnp.transpose(on_first), on_second[:, :128] + on_second[:, 128:]))
    for d, (k, (ga, gb)) in enumerate(zip(ks, sums)):
        ga = ga[0:8] + ga[8:16]
        gb = gb[0:8] + gb[8:16]
        on_a = -0.5 * ga - tiles[buffer, d, 0] * ga[3:4, :]
        on_b = gb - tiles[buffer, d, 1] * gb[5:6, :]
        on_ref[pl.ds(k, 3, stride=2 * PAIRS), :] = on_a[0:3]
        on_ref[pl.ds(PAIRS + k, 3, stride=2 * PAIRS), :] = on_b[0:3]


def kernel(
    count_any, ref_any, disp_any, vel_any, pres_any, cond_any, mask_any, send_any, pair_any, flags_any,
    state,
    pair_s, count_s, ref, disp, vel, pres, cond, mask, send_v, pair_v, flags, rest, shift, speed, chooser, slots_rest, slots_move, on, c1, c2,
    factor, coords, tiles,
    ref_out, ref_in, mov_out0, mov_out1, mov_in0, mov_in1, frc_out0, frc_out1, frc_in0, frc_in1,
    load_out, load_in,
    cells0, cells1, west0, east0, west1, east1, north0, south0, north1, south1,
    face_n, face_s, face_w, face_e, press, wet,
    in_sem, send_sem, recv_sem, halo_send, halo_recv,
):
    s = lax.axis_index("slab")
    u = lax.axis_index("sub")
    slabs = lax.axis_size("slab")
    subs = lax.axis_size("sub")
    y, x = s // SIDE, s % SIDE
    odd = u % 2
    targets, sources = [], []
    for dy, dx in ORDER:
        ty = dy + odd * ((SIDE - dx) % SIDE - dy)
        tx = dx + odd * (dy - dx)
        targets.append(((y + ty) % SIDE) * SIDE + (x + tx) % SIDE)
        sources.append(((y + SIDE - ty) % SIDE) * SIDE + (x + SIDE - tx) % SIDE)
    up, down = (s + slabs - 1) % slabs, (s + 1) % slabs
    left, right = (u + subs - 1) % subs, (u + 1) % subs

    loads = []
    for n, (src, dst) in enumerate(
        (
            (send_any, send_v), (ref_any, ref), (disp_any, disp), (vel_any, vel), (pres_any, pres),
            (mask_any, mask), (cond_any, cond), (pair_any, pair_v), (pair_any, pair_s), (count_any, count_s),
            (flags_any, flags),
        )
    ):
        loads.append(pltpu.make_async_copy(src, dst, in_sem.at[n]))
        loads[n].start()

    barrier = pltpu.get_barrier_semaphore()
    for target in targets:
        pl.semaphore_signal(barrier, inc=1, device_id=(target, u), device_id_type=MESH)
    for v in (left, right):
        pl.semaphore_signal(barrier, inc=1, device_id=(s, v), device_id_type=MESH)

    def gather_blocks(pairs_of_refs):
        for l in range(NB):
            for src, dst in pairs_of_refs:
                dst[pl.ds(l, 3, stride=NB), :] = src[:, 128 * l : 128 * l + 128]

    def fields(buffer):
        return [buffer[f * NB : (f + 1) * NB, :] for f in range(3)]

    def placed():
        return [r + d for r, d in zip(fields(rest), fields(shift))]

    def load_of(pressure):
        return 0.5 + (0.5 * COUPLING) * (pressure * wet[...])

    def start(src, dst, phase, part):
        copies = []
        for n in part:
            copy = pltpu.make_async_remote_copy(
                src_ref=src.at[targets[n]],
                dst_ref=dst.at[s],
                send_sem=send_sem.at[phase, n],
                recv_sem=recv_sem.at[phase, n],
                device_id=(targets[n], u),
                device_id_type=MESH,
            )
            copy.start()
            copies.append(copy)
        return copies

    def fill(row, picked, dst, count):
        for q in range(SIDE):
            for f in range(count):
                dst[row * SIDE + q, f * CAP : (f + 1) * CAP, :] = picked[
                    q * CAP : (q + 1) * CAP, f * 128 : (f + 1) * 128
                ]

    def by_rows(make_row, src, dst, phase, count, ready=None):
        copies = []
        for step in (0, 1, 3, 2):
            row = (y + step) % SIDE
            fill(row, make_row(row), src, count)
            if step == 3:
                if ready is not None:
                    ready()
                copies += start(src, dst, phase, range(NEAR))
        return copies + start(src, dst, phase, range(NEAR, len(ORDER)))

    def chosen_rows(values):
        parts = split(jnp.concatenate(values, axis=1))

        def make_row(row):
            pick = chooser[pl.ds(pl.multiple_of(row * SIDE * CAP, SIDE * CAP), SIDE * CAP), :]
            return dot(pick, parts[0]) + dot(pick, parts[1]) + dot(pick, parts[2])

        return make_row

    def place(src, dst, p, first, count):
        for f in range(count):
            for g in range(CAP // 8):
                dst[pl.ds(p * CAP + 8 * g, 8), first + f, :] = src[
                    p, pl.ds(f * CAP + 8 * g, 8), :
                ]

    def receive(copies, own, src, dst, first, count):
        place(own, dst, s, first, count)
        for copy, p in zip(copies, sources):
            copy.wait_recv()
            place(src, dst, p, first, count)

    def halo(src, n, dev, dst):
        return pltpu.make_async_remote_copy(
            src_ref=src, dst_ref=dst, send_sem=halo_send.at[n], recv_sem=halo_recv.at[n],
            device_id=dev, device_id_type=MESH,
        )

    rows = lax.broadcasted_iota(jnp.int32, (64, 128), 0)
    lanes = lax.broadcasted_iota(jnp.int32, (64, 128), 1)

    def neighbours(centre, north, south, west, east):
        return (
            jnp.where(rows == 0, north[7:8, :], pltpu.roll(centre, 1, 0)),
            jnp.where(rows == 63, south[0:1, :], pltpu.roll(centre, 63, 0)),
            jnp.where(lanes == 0, pltpu.roll(west, 1, 1), pltpu.roll(centre, 1, 1)),
            jnp.where(lanes == 127, pltpu.roll(east, 127, 1), pltpu.roll(centre, 127, 1)),
        )

    def faces():
        inside = (
            jnp.logical_or(rows > 0, s > 0),
            jnp.logical_or(rows < 63, s < slabs - 1),
            jnp.logical_or(lanes > 0, u > 0),
            jnp.logical_or(lanes < 127, u < subs - 1),
        )
        wets = neighbours(wet[...], north0[1], south0[1], west0[1], east0[1])
        rocks = neighbours(cells0[2], north0[2], south0[2], west0[2], east0[2])
        for face, ok, w, r in zip((face_n, face_s, face_w, face_e), inside, wets, rocks):
            value = 0.5 * (cond[...] * wet[...] * w + r * wet[...])
            face[...] = jnp.where(ok, value, 0.0)

    def flow(north, south, west, east):
        centre = press[...]
        total = jnp.zeros_like(centre)
        around = neighbours(centre, north, south, west, east)
        for face, value in zip((face_s, face_n, face_e, face_w), (1, 0, 3, 2)):
            total = total + face[...] * (around[value] - centre)
        press[...] = centre + FLOW * total

    def pair_forces():
        def members(j):
            return [j * GROUP + d for d in range(GROUP)]

        def make(buffer, j):
            bond_factors(buffer, members(j), pair_s, slots_move, c1, c2, factor, coords, tiles)

        def add(buffer, j):
            bond_sums(buffer, members(j), on, factor, coords, tiles)

        groups = PAIRS // GROUP
        make(0, 0)

        @pl.loop(0, groups // 2 - 1)
        def _(i):
            add(0, 2 * i)
            make(1, 2 * i + 1)
            add(1, 2 * i + 1)
            make(0, 2 * i + 2)

        add(0, groups - 2)
        make(1, groups - 1)
        add(1, groups - 1)

    def give_back(src, dst, phase):
        live = lax.broadcasted_iota(jnp.int32, (2, PAIRS), 1) < count_s[0]
        named = jnp.where(live, pair_v[...], -1)
        ends = jnp.concatenate([named[0:1, :], named[1:2, :]], axis=1)
        parts = split(
            jnp.concatenate([on[f * 2 * PAIRS : (f + 1) * 2 * PAIRS, :] for f in range(3)], axis=1)
        )

        def make_row(row):
            slot = lax.broadcasted_iota(jnp.int32, (SIDE * CAP, 2 * PAIRS), 0) + row * (SIDE * CAP)
            hit = jnp.where(slot == ends, 1.0, 0.0).astype(BF16)
            return dot(hit, parts[0]) + dot(hit, parts[1])

        return by_rows(make_row, src, dst, phase, 3)

    def force_from(src, p):
        parts = split(jnp.concatenate([src[p, f * CAP : (f + 1) * CAP, :] for f in range(3)], axis=1))
        pick = chooser[pl.ds(pl.multiple_of(p * CAP, CAP), CAP), :]
        return dot(pick, parts[0], 0, 0) + dot(pick, parts[1], 0, 0)

    def advance(copies, own, src):
        force = force_from(own, s)
        for copy, p in zip(copies, sources):
            copy.wait_recv()
            force = force + force_from(src, p)
        for f in range(3):
            part = slice(f * NB, (f + 1) * NB)
            v = speed[part, :] + (DT * FORCE_SCALE) * force[:, f * 128 : (f + 1) * 128]
            speed[part, :] = v
            shift[part, :] = shift[part, :] + DT * v

    for copy in loads[:2]:
        copy.wait()
    gather_blocks([(ref, rest)])
    chosen = jnp.concatenate([send_v[p : p + 1, :] for p in range(PEERS)], axis=1)
    block = lax.broadcasted_iota(jnp.int32, (NB, PEERS * CAP), 0)
    table = jnp.where(chosen == block, 1.0, 0.0)
    chooser[...] = jnp.transpose(table).astype(BF16)
    rest_copies = by_rows(
        chosen_rows(fields(rest)), ref_out, ref_in, 0, 3,
        lambda: pl.semaphore_wait(barrier, len(ORDER) + 2),
    )

    for copy in loads[2:7]:
        copy.wait()
    gather_blocks([(disp, shift), (vel, speed)])
    wet[...] = mask[...].astype(F32)
    press[...] = pres[...]
    make_row = chosen_rows(placed() + [load_of(press[...])])
    for row in range(SIDE):
        fill(row, make_row(row), mov_out0, 4)
    cells0[0] = pres[...]
    cells0[1] = wet[...]
    cells0[2] = cond[...] * wet[...]
    for copy in rest_copies:
        copy.wait_send()
    move_copies = start(mov_out0, mov_in0, 1, range(len(ORDER)))
    halos = [
        halo(cells0.at[:, pl.ds(56, 8)], 0, (down, u), north0),
        halo(cells0.at[:, pl.ds(0, 8)], 1, (up, u), south0),
        halo(cells0, 2, (s, right), west0),
        halo(cells0, 3, (s, left), east0),
    ]
    for copy in halos:
        copy.start()
    slots_rest[...] = jnp.zeros_like(slots_rest)
    slots_move[...] = jnp.zeros_like(slots_move)

    receive(rest_copies, ref_out, ref_in, slots_rest, 0, 3)
    for copy in loads[7:]:
        copy.wait()

    @pl.loop(0, PAIRS // REST_GROUP)
    def _(j):
        rest_group(
            [j * REST_GROUP + d for d in range(REST_GROUP)], pair_s, slots_rest, flags, c1, c2
        )

    for copy in halos:
        copy.wait_recv()
    faces()
    flow(north0[0], south0[0], west0[0], east0[0])
    make_row = chosen_rows([load_of(press[...])])
    for row in range(SIDE):
        fill(row, make_row(row), load_out, 1)
    receive(move_copies, mov_out0, mov_in0, slots_move, 0, 4)
    load_copies = start(load_out, load_in, 3, range(len(ORDER)))
    cells1[...] = press[...]
    halos1 = [
        halo(cells1.at[pl.ds(56, 8)], 4, (down, u), north1),
        halo(cells1.at[pl.ds(0, 8)], 5, (up, u), south1),
        halo(cells1, 6, (s, right), west1),
        halo(cells1, 7, (s, left), east1),
    ]
    for copy in halos1:
        copy.start()

    pair_forces()
    back_copies = give_back(frc_out0, frc_in0, 2)
    receive(load_copies, load_out, load_in, slots_move, 3, 1)
    for copy in halos1:
        copy.wait_recv()
    flow(north1[...], south1[...], west1[...], east1[...])
    state[6 * NB :, :] = press[...]
    advance(back_copies, frc_out0, frc_in0)

    next_copies = by_rows(chosen_rows(placed()), mov_out1, mov_in1, 4, 3)
    receive(next_copies, mov_out1, mov_in1, slots_move, 0, 3)
    pair_forces()
    last_copies = give_back(frc_out1, frc_in1, 5)
    advance(last_copies, frc_out1, frc_in1)
    state[0 : 3 * NB, :] = shift[...]
    state[3 * NB : 6 * NB, :] = speed[...]
    for copies in (move_copies, halos, load_copies, halos1, back_copies, next_copies, last_copies):
        for copy in copies:
            copy.wait_send()


def unpack_kernel(state, disp_o, vel_o, pres_o):
    for l in range(NB):
        lanes = slice(128 * l, 128 * l + 128)
        disp_o[:, lanes] = state[pl.ds(l, 3, stride=NB), :]
        vel_o[:, lanes] = state[pl.ds(3 * NB + l, 3, stride=NB), :]
    pres_o[...] = state[6 * NB :, :]


def body(ref_pos, disp, vel, pressure, conductivity, frac_mask, send_list, pair_list, pair_count, bond_flags):
    vmem = pl.BlockSpec(memory_space=pltpu.VMEM)
    pairs = pair_list.T
    grid = pltpu.VMEM((64, 128), F32)
    whole = pltpu.VMEM((64, 128), jnp.int32)
    wide = pltpu.VMEM((3, NB * 128), F32)
    three = pltpu.VMEM((3 * NB, 128), F32)
    third = pltpu.VMEM((PEERS, 3 * CAP, 128), F32)
    first = pltpu.VMEM((PEERS, CAP, 128), F32)
    fourth = pltpu.VMEM((PEERS, 4 * CAP, 128), F32)
    slots = pltpu.VMEM((PEERS * CAP, 8, 128), F32)
    grids = pltpu.VMEM((3, 64, 128), F32)
    strips = pltpu.VMEM((3, 8, 128), F32)
    strip = pltpu.VMEM((8, 128), F32)
    bonds = pltpu.VMEM((PAIRS, 128, 128), F32)
    state = pl.pallas_call(
        kernel,
        out_shape=jax.ShapeDtypeStruct((7 * NB, 128), F32),
        in_specs=[pl.BlockSpec(memory_space=pl.ANY)] * 10,
        out_specs=vmem,
        scratch_shapes=[
            pltpu.SMEM((2, PAIRS), jnp.int32), pltpu.SMEM((1,), jnp.int32),
            wide, wide, wide, grid, grid, whole, pltpu.VMEM((PEERS, CAP), jnp.int32), pltpu.VMEM((2, PAIRS), jnp.int32),
            pltpu.VMEM((10, PAIRS, 128), jnp.int32),
            three, three, three,
            pltpu.VMEM((PEERS * CAP, NB), BF16),
            slots, slots,
            pltpu.VMEM((3 * 2 * PAIRS, 128), F32),
            bonds, bonds,
            pltpu.VMEM((2, GROUP, 2, 128, 128), BF16),
            pltpu.VMEM((2, GROUP, 2, 16, 128), BF16),
            pltpu.VMEM((2, GROUP, 2, 8, 128), F32),
            third, third, fourth, third, fourth, third, third, third, third, third, first, first,
            grids, grid, grids, grids, grid, grid, strips, strips, strip, strip,
            grid, grid, grid, grid, grid, grid,
            pltpu.SemaphoreType.DMA((11,)),
            pltpu.SemaphoreType.DMA((6, PEERS)),
            pltpu.SemaphoreType.DMA((6, PEERS)),
            pltpu.SemaphoreType.DMA((8,)),
            pltpu.SemaphoreType.DMA((8,)),
        ],
        compiler_params=pltpu.CompilerParams(
            collective_id=0, has_side_effects=True, vmem_limit_bytes=58 << 20
        ),
    )(
        pair_count, ref_pos, disp, vel, pressure, conductivity, frac_mask, send_list, pairs,
        bond_flags.transpose(1, 0, 2),
    )
    return pl.pallas_call(
        unpack_kernel,
        out_shape=(
            jax.ShapeDtypeStruct(disp.shape, F32),
            jax.ShapeDtypeStruct(vel.shape, F32),
            jax.ShapeDtypeStruct(pressure.shape, F32),
        ),
        in_specs=[vmem],
        out_specs=(vmem, vmem, vmem),
    )(state)


def solution(mesh):
    in_specs = (
        P(None, ("slab", "sub")),
        P(None, ("slab", "sub")),
        P(None, ("slab", "sub")),
        P("slab", "sub"),
        P("slab", "sub"),
        P("slab", "sub"),
        P(("slab", "sub"), None),
        P(("slab", "sub"), None),
        P(("slab", "sub")),
        P(("slab", "sub"), None, None),
    )
    out_specs = (P(None, ("slab", "sub")), P(None, ("slab", "sub")), P("slab", "sub"))
    return jax.shard_map(body, mesh=mesh, in_specs=in_specs, out_specs=out_specs, check_vma=False)
```
